128 devices in a mesh: rows: 8 (over y, core), cols: 16 (over x, z).
Axes of the slice: x: 4, y: 4, z: 4, core: 2. Of those that a mesh axis runs over, the one named last changes fastest.
Arguments:
- lot_features: bfloat16 [16384, 512], P(('rows', 'cols')), may hold values from -60 to 60
- slot_features: bfloat16 [16384, 512], P(('cols', 'rows')), may hold values from -60 to 60
- lot_mass: float32 [16384], P('rows'), may hold values from 0.5 to 2
- slot_mass: float32 [16384], P('cols'), may hold values from 0.5 to 2
Outputs:
- lot_grad: float32 [16384, 512], P(('rows', 'cols'))
The draws below stay inside these ranges and needn't reach their ends.
All inputs are finite; a program needn't handle non-finite values.
Results may differ from the reference program's by a relative error of at most 0.0034.
Values may be sent and summed in bfloat16 or wider, within the bound.
No kernel may reach another device: no remote copies, remote signals or barrier semaphores. Data moves between devices by JAX's collectives and lax.ppermute only.
A program may use at most 64 MiB of HBM per device.

```python
import math
import jax
import jax.numpy as jnp
from jax import lax

F = 512
ITERS = 3
LOT_DEV = 2048
N = 16384
M = 16384
N_ROWS = 8


def far_rows(key, count):
    pick_key = jax.random.fold_in(key, 1)
    one_key = jax.random.fold_in(key, 2)
    chance = jax.random.uniform(pick_key, (count,), jnp.float32) < 0.1
    forced = jnp.arange(count) == jax.random.randint(one_key, (), 0, count)
    return jnp.logical_or(chance, forced)


def feature_rows(key, count, width, hidden_spread):
    values = jnp.clip(jax.random.normal(jax.random.fold_in(key, 3), (count, width), jnp.float32), -6.0, 6.0)
    far = far_rows(key, count)
    scales = jnp.exp(jax.random.uniform(jax.random.fold_in(key, 4), (count,), jnp.float32, 0.0, hidden_spread))
    factor = jnp.where(far, 10.0, scales)
    return (values * factor[:, None]).astype(jnp.bfloat16)


def draw_lot_features(key, part):
    key = jax.random.fold_in(key, 11)
    return feature_rows(key, N, F, 0.0)


def draw_slot_features(key, part):
    key = jax.random.fold_in(key, 23)
    return feature_rows(key, M, F, 0.0)


def block_levels(own_key, extent, cuts, smallest, top_value):
    level, own = 1.0, jax.random.fold_in(own_key, 6)
    for dim, shards_of in cuts:
        steps = jnp.exp(jax.random.uniform(jax.random.fold_in(own, dim), (shards_of,), jnp.float32, smallest / len(cuts), top_value / len(cuts)))
        level = level * jnp.repeat(steps, extent[dim] // shards_of).reshape([-1 if axis == dim else 1 for axis in range(len(extent))])
    return level


def setup_inputs(seed: int = 0) -> dict:
    key_list = jax.random.split(jax.random.key(seed), 5)
    lot_features = draw_lot_features(jax.random.fold_in(key_list[4], 71), 0)
    slot_features = draw_slot_features(jax.random.fold_in(key_list[4], 71), 0)
    lot_mass = jnp.clip(jnp.exp(math.log(2.0) - 1.3862944 * jax.random.uniform(key_list[2], (N,), jnp.float32) ** block_levels(key_list[2], (N,), ((0, 8),), -0.2, 0.2)), 0.5, 2.0)
    slot_mass = jnp.clip(jnp.exp(math.log(2.0) - 1.3862944 * jax.random.uniform(key_list[3], (M,), jnp.float32) ** block_levels(key_list[3], (M,), ((0, 16),), -0.2, 0.2)), 0.5, 2.0)
    return dict(lot_features=lot_features, slot_features=slot_features, lot_mass=lot_mass, slot_mass=slot_mass)


EPS = 1.0


def cost_block(lot_block, slot_features, slot_sq):
    lot_sq = jnp.sum(lot_block.astype(jnp.float32) ** 2, axis=1)
    inner = lax.dot_general(lot_block, slot_features, (((1,), (1,)), ((), ())), preferred_element_type=jnp.float32)
    return (lot_sq[:, None] + slot_sq[None, :] - 2.0 * inner) * (0.5 / (F ** 0.5))


def reference(lot_features, slot_features, lot_mass, slot_mass):
    slot_sq = jnp.sum(slot_features.astype(jnp.float32) ** 2, axis=1)
    blocks = lot_features.reshape(N_ROWS, LOT_DEV, F)
    log_lot = jnp.log(lot_mass).reshape(N_ROWS, LOT_DEV)
    log_slot = jnp.log(slot_mass)
    slot_pot = jnp.zeros((M,), jnp.float32)
    lot_pot = jnp.zeros((N_ROWS, LOT_DEV), jnp.float32)
    for step in range(ITERS):
        def lot_update(pair):
            block, logs = pair
            scores = (slot_pot[None, :] - cost_block(block, slot_features, slot_sq)) / EPS
            return EPS * logs - EPS * jax.nn.logsumexp(scores, axis=1)

        lot_pot = lax.map(lot_update, (blocks, log_lot))

        def col_part(pair):
            block, pots = pair
            scores = (pots[:, None] - cost_block(block, slot_features, slot_sq)) / EPS
            peaks = jnp.max(scores, axis=0)
            return peaks, jnp.sum(jnp.exp(scores - peaks[None, :]), axis=0)

        peaks, totals = lax.map(col_part, (blocks, lot_pot))
        top = jnp.max(peaks, axis=0)
        whole = jnp.sum(totals * jnp.exp(peaks - top[None, :]), axis=0)
        slot_pot = EPS * log_slot - EPS * (top + jnp.log(whole))

    def grad_block(pair):
        block, pots = pair
        plan = jnp.exp((pots[:, None] + slot_pot[None, :] - cost_block(block, slot_features, slot_sq)) / EPS)
        row_total = jnp.sum(plan, axis=1)
        moved = jnp.dot(plan.astype(jnp.bfloat16), slot_features, preferred_element_type=jnp.float32)
        return row_total[:, None] * block.astype(jnp.float32) - moved

    return lax.map(grad_block, (blocks, lot_pot)).reshape(N, F)
```

```python
import math

import jax
import jax.numpy as jnp
from jax import lax
from jax.experimental import pallas as pl
from jax.experimental.pallas import tpu as pltpu
from jax.sharding import Mesh, PartitionSpec as P

ITERS = 3
LOG2E = math.log2(math.e)
LANES = 128

LOT_GROUP = ("x", "core")
SLOT_GROUP = ("y", "z")


def lane_sum(values):
    total = values[:, :LANES]
    for start in range(LANES, values.shape[1], LANES):
        total = total + values[:, start : start + LANES]
    return jnp.sum(total.T, axis=0, keepdims=True)


def square_row(block):
    wide = block.astype(jnp.float32)
    return lane_sum(wide * wide) * (0.5 * LOG2E / math.sqrt(block.shape[1]))


def joined(parts):
    top = parts[0]
    for part in parts[1:]:
        top = jnp.maximum(top, part)
    total = jnp.exp2(parts[0] - top)
    for part in parts[1:]:
        total = total + jnp.exp2(part - top)
    return top + jnp.log(total) * LOG2E


def row_pass(score, wide_g, peak, total):
    lots, slots = score.shape
    tiles = slots // LANES

    def step(i, carry):
        rows = pl.ds(pl.multiple_of(i * 8, 8), 8)
        terms = [
            score[rows, t * LANES : (t + 1) * LANES] + wide_g[t * 8 : (t + 1) * 8, :]
            for t in range(tiles)
        ]
        top = terms[0]
        for term in terms[1:]:
            top = jnp.maximum(top, term)
        whole = jnp.exp2(terms[0] - top)
        for term in terms[1:]:
            whole = whole + jnp.exp2(term - top)
        peak[rows, :] = top
        total[rows, :] = whole
        return carry

    lax.fori_loop(0, lots // 8, step, 0, unroll=4)


def row_result(peak, total):
    out = []
    for start in range(0, peak.shape[0], LANES):
        tops = peak[start : start + LANES, :].T
        sums = total[start : start + LANES, :].T
        top = jnp.max(tops, axis=0, keepdims=True)
        whole = jnp.sum(sums * jnp.exp2(tops - top), axis=0, keepdims=True)
        out.append(top + jnp.log(whole) * LOG2E)
    return jnp.concatenate(out, axis=0)


def column_pass(score, wide_f):
    lots, slots = score.shape
    out = []
    for t in range(slots // LANES):
        cols = slice(t * LANES, (t + 1) * LANES)

        def terms_of(start):
            return [
                score[pl.ds(start + k, 8), cols] + wide_f[pl.ds(start + k, 8), :]
                for k in range(0, LANES, 8)
            ]

        def fold(terms, top):
            whole = jnp.exp2(terms[0] - top)
            for term in terms[1:]:
                whole = whole + jnp.exp2(term - top)
            return whole

        def peak_of(terms):
            top = terms[0]
            for term in terms[1:]:
                top = jnp.maximum(top, term)
            return top

        terms = terms_of(0)
        top = peak_of(terms)
        whole = fold(terms, top)
        for start in range(LANES, lots, LANES):
            terms = terms_of(start)
            new = jnp.maximum(top, peak_of(terms))
            whole = whole * jnp.exp2(top - new) + fold(terms, new)
            top = new
        high = jnp.max(top, axis=0, keepdims=True)
        whole = jnp.sum(whole * jnp.exp2(top - high), axis=0, keepdims=True)
        out.append(high + jnp.log(whole) * LOG2E)
    return jnp.concatenate(out, axis=0)


def spread_rows(values, wide):
    for t in range(values.shape[0]):
        wide[t * 8 : (t + 1) * 8, :] = jnp.broadcast_to(values[t : t + 1, :], (8, LANES))


def spread_columns(values, wide):
    for r in range(values.shape[0]):
        wide[r * LANES : (r + 1) * LANES, :] = jnp.broadcast_to(values[r : r + 1, :], (LANES, LANES)).T


def send_out(out, values, copies):
    rows = values.shape[0]
    for n in range(copies):
        out[n * rows : (n + 1) * rows, :] = values


def padded(rows):
    have = jnp.concatenate(rows, axis=0)
    return jnp.concatenate([have, jnp.zeros((8 - have.shape[0], LANES), jnp.float32)], axis=0)


def score_kernel(peers, lots, slots, own_lots, own_mass, score, out, wide_g, peak, total):
    scale = LOG2E / math.sqrt(lots.shape[1])
    step = 256
    for start in range(0, slots.shape[0], step):
        inner = lax.dot_general(
            lots[...], slots[start : start + step, :], (((1,), (1,)), ((), ())), preferred_element_type=jnp.float32
        )
        score[:, start : start + step] = inner * scale
    norms = [square_row(slots[start : start + LANES, :]) for start in range(0, slots.shape[0], LANES)]
    spread_rows(-jnp.concatenate(norms, axis=0), wide_g)
    row_pass(score, wide_g, peak, total)
    own = padded([jnp.log(own_mass[...]) * LOG2E, square_row(own_lots[...])])
    send_out(out, jnp.concatenate([row_result(peak, total), own], axis=0), peers)


def lot_update(parts, first, shares, blocks):
    stride = parts.shape[0] // shares
    log_sum = joined([parts[n * stride : n * stride + blocks, :] for n in range(shares)])
    wide = first.shape[0] // shares
    logs = jnp.concatenate([first[n * wide + blocks : n * wide + blocks + 1, :] for n in range(shares)], axis=0)
    squares = jnp.concatenate([first[n * wide + blocks + 1 : n * wide + blocks + 2, :] for n in range(shares)], axis=0)
    pot = logs + squares - log_sum
    return pot - squares


def slot_update(parts, first, shares, blocks):
    stride = parts.shape[0] // shares
    log_sum = joined([parts[n * stride : n * stride + blocks, :] for n in range(shares)])
    wide = first.shape[0] // shares
    logs = jnp.concatenate([first[n * wide + blocks : n * wide + blocks + 1, :] for n in range(shares)], axis=0)
    return logs - log_sum


def column_kernel(shares, peers, score, parts, first, own_mass, out, f_out, wide_f):
    f = lot_update(parts, first, shares, score.shape[0] // LANES)
    f_out[...] = f
    spread_columns(f, wide_f)
    sums = column_pass(score, wide_f)
    if out.shape[0] // peers > sums.shape[0]:
        sums = jnp.concatenate([sums, padded([jnp.log(own_mass[...]) * LOG2E])], axis=0)
    send_out(out, sums, peers)


def row_kernel(shares, peers, score, parts, first, out, wide_g, peak, total):
    g = slot_update(parts, first, shares, score.shape[1] // LANES)
    spread_rows(g, wide_g)
    row_pass(score, wide_g, peak, total)
    send_out(out, row_result(peak, total), peers)


def final_kernel(shares, score, parts, first, f, lots, slots, out, wide_g, wide_f, plan, row_sum):
    g = slot_update(parts, first, shares, score.shape[1] // LANES)
    spread_rows(g, wide_g)
    spread_columns(f[...], wide_f)
    tiles = score.shape[1] // LANES

    def step(i, carry):
        rows = pl.ds(pl.multiple_of(i * 16, 16), 16)
        shift = wide_f[rows, :]
        whole = None
        for t in range(tiles):
            cols = slice(t * LANES, (t + 1) * LANES)
            both = jnp.concatenate([wide_g[t * 8 : (t + 1) * 8, :]] * 2, axis=0)
            term = jnp.exp2(score[rows, cols] + shift + both)
            plan[rows, cols] = term.astype(jnp.bfloat16)
            whole = term if whole is None else whole + term
        row_sum[rows, :] = jnp.broadcast_to(jnp.sum(whole, axis=1, keepdims=True), whole.shape)
        return carry

    lax.fori_loop(0, score.shape[0] // 16, step, 0, unroll=2)
    step_rows = 256
    for start in range(0, score.shape[0], step_rows):
        rows = slice(start, start + step_rows)
        moved = jnp.dot(plan[rows, :], slots[...], preferred_element_type=jnp.float32)
        sums = jnp.concatenate([row_sum[rows, :]] * (lots.shape[1] // LANES), axis=1)
        out[rows, :] = sums * lots[rows, :].astype(jnp.float32) - moved


def call(kernel, outs, scratch, cost, *args):
    vmem = pl.BlockSpec(memory_space=pltpu.VMEM)
    return pl.pallas_call(
        kernel,
        out_shape=outs,
        in_specs=[vmem] * len(args),
        out_specs=[vmem] * len(outs) if isinstance(outs, (list, tuple)) else vmem,
        scratch_shapes=[pltpu.VMEM(shape, dtype) for shape, dtype in scratch],
        compiler_params=pltpu.CompilerParams(vmem_limit_bytes=40 * 2**20),
        cost_estimate=pl.CostEstimate(flops=cost, bytes_accessed=0, transcendentals=cost // 1024),
    )(*args)


def spread(values, axes):
    return lax.all_to_all(values, axes, 0, 0, tiled=True)


def local(sizes, lot_features, slot_features, lot_mass, slot_mass):
    own_rows, width = lot_features.shape
    lot_share = sizes["x"] * sizes["core"]
    slot_share = sizes["y"] * sizes["z"]
    lot_at = lax.axis_index("x") * sizes["z"] + lax.axis_index("z")
    slot_at = lax.axis_index("y") * sizes["core"] + lax.axis_index("core")
    own_lot_mass = lax.dynamic_slice_in_dim(lot_mass, lot_at * own_rows, own_rows, 0).reshape(1, own_rows)
    own_slot_mass = lax.dynamic_slice_in_dim(slot_mass, slot_at * own_rows, own_rows, 0).reshape(1, own_rows)

    lots = lax.all_gather(lot_features, LOT_GROUP, axis=0, tiled=True)
    slots = spread(jnp.tile(slot_features, (slot_share, 1)), SLOT_GROUP)
    n, m = lots.shape[0], slots.shape[0]
    f32 = jnp.float32

    def shape(*dims):
        return jax.ShapeDtypeStruct(dims, f32)

    wide_g = ((m // LANES * 8, LANES), f32)
    wide_f = ((n, LANES), f32)
    lot_blocks, slot_blocks = n // LANES, m // LANES
    work = n * m * 4

    score, out = call(
        lambda *refs: score_kernel(lot_share, *refs),
        [shape(n, m), shape(lot_share * (lot_blocks + 8), LANES)],
        [wide_g, wide_f, wide_f],
        work,
        lots, slots, lot_features, own_lot_mass,
    )
    first_lot = lot_parts = spread(out, LOT_GROUP)
    first_slot = None
    for step in range(ITERS):
        extra = 8 if step == 0 else 0
        out, f = call(
            lambda *refs: column_kernel(lot_share, slot_share, *refs),
            [shape(slot_share * (slot_blocks + extra), LANES), shape(lot_blocks, LANES)],
            [wide_f],
            work,
            score, lot_parts, first_lot, own_slot_mass,
        )
        slot_parts = spread(out, SLOT_GROUP)
        if step == 0:
            first_slot = slot_parts
        if step < ITERS - 1:
            out = call(
                lambda *refs: row_kernel(slot_share, lot_share, *refs),
                shape(lot_share * lot_blocks, LANES),
                [wide_g, wide_f, wide_f],
                work,
                score, slot_parts, first_slot,
            )
            lot_parts = spread(out, LOT_GROUP)
    grad = call(
        lambda *refs: final_kernel(slot_share, *refs),
        shape(n, width),
        [wide_g, wide_f, ((n, m), jnp.bfloat16), wide_f],
        work,
        score, slot_parts, first_slot, f, lots, slots,
    )
    shares = spread(grad, LOT_GROUP)
    return jnp.sum(shares.reshape(lot_share, own_rows, width), axis=0)


def solution(mesh):
    sizes = {"y": 4, "core": 2, "x": 4, "z": 4}
    fine = Mesh(mesh.devices.reshape(tuple(sizes.values())), tuple(sizes))
    placed = (P(("y", "core", "x", "z"), None), P(("x", "z", "y", "core"), None), P(("y", "core")), P(("x", "z")))
    return jax.shard_map(
        lambda *args: local(sizes, *args), mesh=fine, in_specs=placed, out_specs=P(("y", "core", "x", "z"), None), check_vma=False
    )
```

```python
import math

import jax
import jax.numpy as jnp
from jax import lax
from jax.experimental import pallas as pl
from jax.experimental.pallas import tpu as pltpu
from jax.sharding import Mesh, PartitionSpec as P

ITERS = 3
LOG2E = math.log2(math.e)
LANES = 128

SIZES = {"y": 4, "core": 2, "x": 4, "z": 4}
ALL = tuple(SIZES)
FULL, PAIRS, ACROSS, EACH = [(0, 1, 2, 3)], [(0, 1), (2, 3)], [(1, 2), (3, 0)], [(0,), (1,), (2,), (3,)]


def groups(ys, cores, xs, zs):
    return [
        [((y * 2 + core) * 4 + x) * 4 + z for core in cs for x in px for y in py for z in pz]
        for px in xs
        for py in ys
        for pz in zs
        for cs in cores
    ]


LOT_GROUPS = groups(EACH, [(0,), (1,)], FULL, ACROSS)
SLOT_GROUPS = groups(FULL, [(0, 1)], EACH, PAIRS)
CORE_SLOT_GROUPS = groups(FULL, [(0,), (1,)], EACH, PAIRS)
LOT_SHARE, SLOT_SHARE = 8, 16


def place_in_lots():
    return lax.axis_index("x") * 2 + (lax.axis_index("z") + 1) % 2


def lane_sum(values):
    total = values[:, :LANES]
    for start in range(LANES, values.shape[1], LANES):
        total = total + values[:, start : start + LANES]
    return jnp.sum(total.T, axis=0, keepdims=True)


def square_row(block):
    wide = block.astype(jnp.float32)
    return lane_sum(wide * wide) * (0.5 * LOG2E / math.sqrt(block.shape[1]))


def square_rows(features):
    return jnp.concatenate([square_row(features[start : start + LANES, :]) for start in range(0, features.shape[0], LANES)], axis=0)


def joined(parts):
    top = parts[0]
    for part in parts[1:]:
        top = jnp.maximum(top, part)
    total = jnp.exp2(parts[0] - top)
    for part in parts[1:]:
        total = total + jnp.exp2(part - top)
    return top + jnp.log(total) * LOG2E


def in_pairs(join, terms):
    while len(terms) > 1:
        terms = [join(*terms[i : i + 2]) if i + 1 < len(terms) else terms[i] for i in range(0, len(terms), 2)]
    return terms[0]


def peak_of(terms):
    return in_pairs(jnp.maximum, terms)


def fold(terms, top):
    return in_pairs(jnp.add, [jnp.exp2(term - top) for term in terms])


def onward(state, terms):
    top = peak_of(terms)
    if state is None:
        return top, fold(terms, top)
    top = jnp.maximum(top, state[0])
    return top, state[1] * jnp.exp2(state[0] - top) + fold(terms, top)


def row_pass(scores, wide_g, peak, total, before=None):
    groups_of, tiles_of = 8, 8

    def step(i, carry):
        rows = [pl.ds(pl.multiple_of(i * 8 * groups_of + 8 * r, 8), 8) for r in range(groups_of)]
        states = [None if before is None else (before[0][row, :], before[1][row, :]) for row in rows]
        n = 0
        for score in scores:
            for start in range(0, score.shape[1] // LANES, tiles_of):
                gs = [wide_g[(n + k) * 8 : (n + k + 1) * 8, :] for k in range(tiles_of)]
                n += tiles_of
                for r, row in enumerate(rows):
                    terms = [score[row, (start + k) * LANES : (start + k + 1) * LANES] + g for k, g in enumerate(gs)]
                    states[r] = onward(states[r], terms)
        for row, (top, whole) in zip(rows, states, strict=True):
            peak[row, :] = top
            total[row, :] = whole
        return carry

    lax.fori_loop(0, scores[0].shape[0] // (8 * groups_of), step, 0)


def row_result(peak, total):
    out = []
    for start in range(0, peak.shape[0], LANES):
        tops = peak[start : start + LANES, :].T
        sums = total[start : start + LANES, :].T
        top = jnp.max(tops, axis=0, keepdims=True)
        whole = jnp.sum(sums * jnp.exp2(tops - top), axis=0, keepdims=True)
        out.append(top + jnp.log(whole) * LOG2E)
    return jnp.concatenate(out, axis=0)


def column_pass(score, wide_f, sums, first):
    rows, tiles_of = 64, 8

    def step(i, carry):
        cols = [pl.ds(pl.multiple_of((i * tiles_of + k) * LANES, LANES), LANES) for k in range(tiles_of)]
        states = [None] * tiles_of
        for start in range(0, score.shape[0], rows):
            fs = [wide_f[start + k : start + k + 8, :] for k in range(0, rows, 8)]
            for k, col in enumerate(cols):
                terms = [score[start + 8 * n : start + 8 * n + 8, col] + f for n, f in enumerate(fs)]
                states[k] = onward(states[k], terms)
        for k, (top, whole) in enumerate(states):
            high = jnp.max(top, axis=0, keepdims=True)
            whole = jnp.sum(whole * jnp.exp2(top - high), axis=0, keepdims=True)
            sums[pl.ds(first + i * tiles_of + k, 1), :] = high + jnp.log(whole) * LOG2E
        return carry

    lax.fori_loop(0, score.shape[1] // (LANES * tiles_of), step, 0)


def spread_rows(values, wide):
    for t in range(values.shape[0]):
        wide[t * 8 : (t + 1) * 8, :] = jnp.broadcast_to(values[t : t + 1, :], (8, LANES))


def spread_columns(values, wide):
    for r in range(values.shape[0]):
        wide[r * LANES : (r + 1) * LANES, :] = jnp.broadcast_to(values[r : r + 1, :], (LANES, LANES)).T


def padded(rows):
    have = jnp.concatenate(rows, axis=0)
    return jnp.concatenate([have, jnp.zeros((8 - have.shape[0], LANES), jnp.float32)], axis=0)


def fill_scores(lots, slots, score):
    scale = LOG2E / math.sqrt(lots.shape[1])
    step = 256
    for start in range(0, slots.shape[0], step):
        inner = lax.dot_general(
            lots[...], slots[start : start + step, :], (((1,), (1,)), ((), ())), preferred_element_type=jnp.float32
        )
        score[:, start : start + step] = inner * scale


def own_score_kernel(slots, *refs):
    blocks, (lots, score, peak, total, wide_g, sems) = refs[:2], refs[2:]
    own_rows = lots.shape[0] // LOT_SHARE
    me = place_in_lots()
    copies = []
    for d in range(LOT_SHARE):
        rows = pl.ds(pl.multiple_of((me ^ d) * own_rows, own_rows), own_rows)
        block = blocks[d % 2].at[pl.ds((d // 2) * own_rows, own_rows), :]
        copies.append(pltpu.make_async_copy(block, lots.at[rows, :], sems.at[d]))
    for copy in copies:
        copy.start()
    spread_rows(-square_rows(slots), wide_g)
    for copy in copies:
        copy.wait()
    fill_scores(lots, slots, score)
    row_pass([score], wide_g, peak, total)


def other_score_kernel(slots, lots, peak_before, total_before, own_mass, score, out, wide_g, peak, total):
    spread_rows(-square_rows(slots), wide_g)
    fill_scores(lots, slots, score)
    row_pass([score], wide_g, peak, total, (peak_before, total_before))
    own_rows = own_mass.shape[1]
    own_lots = lots[pl.ds(pl.multiple_of(place_in_lots() * own_rows, own_rows), own_rows), :]
    own = padded([jnp.log(own_mass[...]) * LOG2E, square_row(own_lots)])
    sums = jnp.concatenate([row_result(peak, total), own], axis=0)
    for n in range(LOT_SHARE):
        out[n * sums.shape[0] : (n + 1) * sums.shape[0], :] = sums


def row_of_each(gathered, shares, row):
    stride = gathered.shape[0] // shares
    return [gathered[n * stride + row : n * stride + row + 1, :] for n in range(shares)]


def log_sum_of(parts, shares, blocks):
    stride = parts.shape[0] // shares
    return joined([parts[n * stride : n * stride + blocks, :] for n in range(shares)])


def lot_update(parts, first, blocks):
    logs = jnp.concatenate(row_of_each(first, LOT_SHARE, blocks), axis=0)
    squares = jnp.concatenate(row_of_each(first, LOT_SHARE, blocks + 1), axis=0)
    pot = logs + squares - log_sum_of(parts, LOT_SHARE, blocks)
    return pot - squares


def own_core_first(halves):
    mine, other = halves if isinstance(halves, tuple) else (halves[:8, :], halves[8:, :])
    ahead = lax.axis_index("core") == 0
    return jnp.concatenate([jnp.where(ahead, mine, other), jnp.where(ahead, other, mine)], axis=0)


def slot_update(parts, first, blocks):
    logs = own_core_first(jnp.concatenate(row_of_each(first, SLOT_SHARE, blocks), axis=0))
    return logs - log_sum_of(parts, SLOT_SHARE, blocks)


def column_kernel(score_a, score_b, parts, first, own_mass, out, wide_f, sums):
    spread_columns(lot_update(parts, first, score_a.shape[0] // LANES), wide_f)
    column_pass(score_a, wide_f, sums, 0)
    column_pass(score_b, wide_f, sums, score_a.shape[1] // LANES)
    half = sums.shape[0] // 2
    mine, other = sums[:half, :], sums[half:, :]
    ahead = lax.axis_index("core") == 0
    extra = [padded([jnp.log(own_mass[...]) * LOG2E])] if out.shape[0] // SLOT_SHARE > sums.shape[0] else []
    same = jnp.concatenate([mine, other, *extra], axis=0)
    turned = jnp.concatenate([other, mine, *extra], axis=0)
    rows = same.shape[0]
    for n in range(SLOT_SHARE):
        low = n < SLOT_SHARE // 2
        out[n * rows : (n + 1) * rows, :] = jnp.where(ahead, same if low else turned, turned if low else same)


def row_kernel(score_a, score_b, parts, first, out, wide_g, peak, total):
    spread_rows(slot_update(parts, first, sum_tiles(score_a, score_b)), wide_g)
    row_pass([score_a, score_b], wide_g, peak, total)
    sums = row_result(peak, total)
    for n in range(LOT_SHARE):
        out[n * sums.shape[0] : (n + 1) * sums.shape[0], :] = sums


def sum_tiles(score_a, score_b):
    return (score_a.shape[1] + score_b.shape[1]) // LANES


def final_kernel(score_a, score_b, parts, first, wide_f, lots, slots_a, slots_b, out, wide_g, plan, row_sum):
    spread_rows(slot_update(parts, first, sum_tiles(score_a, score_b)), wide_g)

    def step(i, carry):
        rows = pl.ds(pl.multiple_of(i * 16, 16), 16)
        shift = wide_f[rows, :]
        whole = None
        n = 0
        for score in (score_a, score_b):
            for t in range(score.shape[1] // LANES):
                both = jnp.concatenate([wide_g[n * 8 : (n + 1) * 8, :]] * 2, axis=0)
                term = jnp.exp2(score[rows, t * LANES : (t + 1) * LANES] + shift + both)
                plan[rows, n * LANES : (n + 1) * LANES] = term.astype(jnp.bfloat16)
                whole = term if whole is None else whole + term
                n += 1
        row_sum[rows, :] = jnp.broadcast_to(jnp.sum(whole, axis=1, keepdims=True), whole.shape)
        return carry

    lax.fori_loop(0, plan.shape[0] // 16, step, 0, unroll=2)
    half = score_a.shape[1]
    step_cols = 256
    for start in range(0, lots.shape[1], step_cols):
        cols = slice(start, start + step_cols)
        moved = jnp.dot(plan[:, :half], slots_a[:, cols], preferred_element_type=jnp.float32)
        moved = moved + jnp.dot(plan[:, half:], slots_b[:, cols], preferred_element_type=jnp.float32)
        sums = jnp.concatenate([row_sum[...]] * (step_cols // LANES), axis=1)
        out[:, cols] = (sums * lots[:, cols].astype(jnp.float32) - moved).astype(out.dtype)


def call(kernel, outs, scratch, cost, *args, grant=12, far_args=0):
    near, far = pl.BlockSpec(memory_space=pltpu.VMEM), pl.BlockSpec(memory_space=pltpu.HBM)
    return pl.pallas_call(
        kernel,
        out_shape=outs,
        in_specs=[near] * (len(args) - far_args) + [far] * far_args,
        out_specs=[near] * len(outs),
        scratch_shapes=[pltpu.VMEM(*item) if isinstance(item, tuple) else item for item in scratch],
        compiler_params=pltpu.CompilerParams(vmem_limit_bytes=grant * 2**20),
        cost_estimate=pl.CostEstimate(flops=cost, bytes_accessed=0, transcendentals=cost // 1024),
    )(*args)


def exchange(values, members):
    return lax.all_to_all(values, ALL, 0, 0, tiled=True, axis_index_groups=members)


def to_place(values, d):
    return lax.ppermute(values, ALL, [(group[i], group[i ^ d]) for group in LOT_GROUPS for i in range(LOT_SHARE)])


def local(lot_features, slot_features, lot_mass, slot_mass):
    own_rows, width = lot_features.shape
    lot_at = lax.axis_index("x") * SIZES["z"] + lax.axis_index("z")
    slot_at = lax.axis_index("y") * SIZES["core"] + lax.axis_index("core")
    own_lot_mass = lax.dynamic_slice_in_dim(lot_mass, lot_at * own_rows, own_rows, 0).reshape(1, own_rows)
    own_slot_mass = lax.dynamic_slice_in_dim(slot_mass, slot_at * own_rows, own_rows, 0).reshape(1, own_rows)

    core_share = SLOT_SHARE // 2
    slots_a = exchange(jnp.tile(slot_features, (core_share, 1)), CORE_SLOT_GROUPS)
    near = jnp.concatenate([lot_features] + [to_place(lot_features, d) for d in range(2, LOT_SHARE, 2)], axis=0)
    blocks = [near, to_place(near, 1)]
    slots_a, blocks = lax.optimization_barrier((slots_a, blocks))
    slots_b = lax.ppermute(slots_a, "core", [(0, 1), (1, 0)])

    n, half = LOT_SHARE * own_rows, core_share * own_rows
    lot_blocks, slot_blocks = n // LANES, 2 * half // LANES
    f32 = jnp.float32

    def shape(*dims, dtype=f32):
        return jax.ShapeDtypeStruct(dims, dtype)

    wide_g, half_g = ((slot_blocks * 8, LANES), f32), ((slot_blocks * 4, LANES), f32)
    wide_f = ((n, LANES), f32)
    work = n * half * 8

    lots, score_a, peak, total = call(
        own_score_kernel,
        [shape(n, width, dtype=lot_features.dtype), shape(n, half), shape(n, LANES), shape(n, LANES)],
        [half_g, pltpu.SemaphoreType.DMA((LOT_SHARE,))],
        work,
        slots_a, *blocks, far_args=2,
    )
    score_b, out = call(
        other_score_kernel,
        [shape(n, half), shape(LOT_SHARE * (lot_blocks + 8), LANES)],
        [half_g, wide_f, wide_f],
        work,
        slots_b, lots, peak, total, own_lot_mass,
    )
    out, own_slot_mass = lax.optimization_barrier((out, own_slot_mass))
    first_lot = lot_parts = exchange(out, LOT_GROUPS)
    first_slot = None
    for step in range(ITERS):
        extra = 8 if step == 0 else 0
        out, f = call(
            column_kernel,
            [shape(SLOT_SHARE * (slot_blocks + extra), LANES), shape(n, LANES)],
            [((slot_blocks, LANES), f32)],
            work,
            score_a, score_b, lot_parts, first_lot, own_slot_mass,
        )
        slot_parts = exchange(out, SLOT_GROUPS)
        if step == 0:
            first_slot = slot_parts
        if step < ITERS - 1:
            (out,) = call(
                row_kernel,
                [shape(LOT_SHARE * lot_blocks, LANES)],
                [wide_g, wide_f, wide_f],
                work,
                score_a, score_b, slot_parts, first_slot,
            )
            lot_parts = exchange(out, LOT_GROUPS)

    (partial,) = call(
        final_kernel,
        [shape(n, width, dtype=jnp.bfloat16)],
        [wide_g, ((n, 2 * half), jnp.bfloat16), wide_f],
        work,
        score_a, score_b, slot_parts, first_slot, f, lots, slots_a, slots_b,
    )
    shares = exchange(partial, LOT_GROUPS).astype(f32)
    return jnp.sum(shares.reshape(LOT_SHARE, own_rows, width), axis=0)


def solution(mesh):
    fine = Mesh(mesh.devices.reshape(tuple(SIZES.values())), ALL)
    placed = (P(ALL, None), P(("x", "z", "y", "core"), None), P(("y", "core")), P(("x", "z")))
    return jax.shard_map(local, mesh=fine, in_specs=placed, out_specs=P(ALL, None), check_vma=False)
```

```python
import math

import jax
import jax.numpy as jnp
from jax import lax
from jax.experimental import pallas as pl
from jax.experimental.pallas import tpu as pltpu
from jax.sharding import Mesh, PartitionSpec as P

ITERS = 3
LOG2E = math.log2(math.e)
LANES = 128

SIZES = {"y": 4, "core": 2, "x": 4, "z": 4}
ALL = tuple(SIZES)
FULL, PAIRS, ACROSS, EACH = [(0, 1, 2, 3)], [(0, 1), (2, 3)], [(1, 2), (3, 0)], [(0,), (1,), (2,), (3,)]


def groups(ys, cores, xs, zs):
    return [
        [((y * 2 + core) * 4 + x) * 4 + z for core in cs for x in px for y in py for z in pz]
        for px in xs
        for py in ys
        for pz in zs
        for cs in cores
    ]


LOT_GROUPS = groups(EACH, [(0,), (1,)], FULL, PAIRS)
SLOT_GROUPS = groups(FULL, [(0, 1)], EACH, ACROSS)
CORE_SLOT_GROUPS = groups(FULL, [(0,), (1,)], EACH, ACROSS)
LOT_SHARE, SLOT_SHARE = 8, 16
CHUNKS = 2


def place_in_lots():
    return lax.axis_index("x") * 2 + lax.axis_index("z") % 2


def lane_sum(values):
    total = values[:, :LANES]
    for start in range(LANES, values.shape[1], LANES):
        total = total + values[:, start : start + LANES]
    return jnp.sum(total.T, axis=0, keepdims=True)


def square_row(block):
    wide = block.astype(jnp.float32)
    return lane_sum(wide * wide) * (0.5 * LOG2E / math.sqrt(block.shape[1]))


def square_rows(features):
    return jnp.concatenate([square_row(features[start : start + LANES, :]) for start in range(0, features.shape[0], LANES)], axis=0)


def joined(parts):
    top = parts[0]
    for part in parts[1:]:
        top = jnp.maximum(top, part)
    total = jnp.exp2(parts[0] - top)
    for part in parts[1:]:
        total = total + jnp.exp2(part - top)
    return top + jnp.log(total) * LOG2E


def in_pairs(join, terms):
    while len(terms) > 1:
        terms = [join(*terms[i : i + 2]) if i + 1 < len(terms) else terms[i] for i in range(0, len(terms), 2)]
    return terms[0]


def peak_of(terms):
    return in_pairs(jnp.maximum, terms)


def fold(terms, top):
    return in_pairs(jnp.add, [jnp.exp2(term - top) for term in terms])


def onward(state, terms):
    top = peak_of(terms)
    if state is None:
        return top, fold(terms, top)
    top = jnp.maximum(top, state[0])
    return top, state[1] * jnp.exp2(state[0] - top) + fold(terms, top)


def row_pass(score, wide_g, peak, total, first):
    groups_of, tiles_of = 8, 8

    def step(i, carry):
        rows = [pl.multiple_of(i * 8 * groups_of + 8 * r, 8) for r in range(groups_of)]
        states = [None] * groups_of
        for start in range(0, score.shape[1] // LANES, tiles_of):
            gs = [wide_g[(start + k) * 8 : (start + k + 1) * 8, :] for k in range(tiles_of)]
            for r, row in enumerate(rows):
                terms = [score[pl.ds(row, 8), (start + k) * LANES : (start + k + 1) * LANES] + g for k, g in enumerate(gs)]
                states[r] = onward(states[r], terms)
        for row, (top, whole) in zip(rows, states, strict=True):
            peak[pl.ds(first + row, 8), :] = top
            total[pl.ds(first + row, 8), :] = whole
        return carry

    lax.fori_loop(0, score.shape[0] // (8 * groups_of), step, 0)


def row_result(peak, total):
    out = []
    for start in range(0, peak.shape[0], LANES):
        tops = peak[start : start + LANES, :].T
        sums = total[start : start + LANES, :].T
        top = jnp.max(tops, axis=0, keepdims=True)
        whole = jnp.sum(sums * jnp.exp2(tops - top), axis=0, keepdims=True)
        out.append(top + jnp.log(whole) * LOG2E)
    return jnp.concatenate(out, axis=0)


def column_pass(scores, wide_f, sums):
    rows, tiles_of = 64, 8
    below = scores[0].shape[0]

    def step(i, carry):
        cols = [pl.ds(pl.multiple_of((i * tiles_of + k) * LANES, LANES), LANES) for k in range(tiles_of)]
        states = [None] * tiles_of
        for start in range(0, wide_f.shape[0], rows):
            score, at = scores[start // below], start % below
            fs = [wide_f[start + k : start + k + 8, :] for k in range(0, rows, 8)]
            for k, col in enumerate(cols):
                terms = [score[at + 8 * n : at + 8 * n + 8, col] + f for n, f in enumerate(fs)]
                states[k] = onward(states[k], terms)
        for k, (top, whole) in enumerate(states):
            high = jnp.max(top, axis=0, keepdims=True)
            whole = jnp.sum(whole * jnp.exp2(top - high), axis=0, keepdims=True)
            sums[pl.ds(i * tiles_of + k, 1), :] = high + jnp.log(whole) * LOG2E
        return carry

    lax.fori_loop(0, sums.shape[0] // tiles_of, step, 0)


def spread_rows(values, wide):
    for t in range(values.shape[0]):
        wide[t * 8 : (t + 1) * 8, :] = jnp.broadcast_to(values[t : t + 1, :], (8, LANES))


def padded(rows):
    have = jnp.concatenate(rows, axis=0)
    return jnp.concatenate([have, jnp.zeros((8 - have.shape[0], LANES), jnp.float32)], axis=0)


def fill_scores(lots, slots, score, first):
    scale = LOG2E / math.sqrt(lots.shape[1])
    step = 256
    for start in range(0, slots.shape[0], step):
        inner = lax.dot_general(
            lots[...], slots[start : start + step, :], (((1,), (1,)), ((), ())), preferred_element_type=jnp.float32
        )
        score[:, first + start : first + start + step] = inner * scale


STEPS = (0, 2, 4, 6, 1, 3, 5, 7)


def to_places(rows, placed, blocks):
    me = place_in_lots()
    for n, b in enumerate(blocks):
        placed[pl.ds(me ^ STEPS[b], 1), :] = rows[n : n + 1, :]


def send_to_lots(values, out):
    rows = values.shape[0]
    for n in range(LOT_SHARE):
        out[n * rows : (n + 1) * rows, :] = values


def gather_rows(parts, lots):
    rows = parts[0].shape[0]
    for n, part in enumerate(parts):
        lots[n * rows : (n + 1) * rows, :] = part[...]


def own_kernel(lots, lot_mass, slot_mass, own_lots, lot_rows, slot_rows):
    own_lots[...] = lots[...]
    masses = lot_mass[pl.ds(lax.axis_index("x") * SIZES["z"] + lax.axis_index("z"), 1), :]
    lot_rows[...] = padded([jnp.log(masses) * LOG2E, square_row(lots[...])])
    masses = slot_mass[pl.ds(lax.axis_index("y") * SIZES["core"] + lax.axis_index("core"), 1), :]
    slot_rows[...] = padded([jnp.log(masses) * LOG2E])


def near_score_kernel(slots_a, slots_b, lot_rows, *refs):
    parts, (score, near, wide_g, placed, peak, total) = refs[: LOT_SHARE // 2], refs[LOT_SHARE // 2 :]
    gather_rows(parts, near)
    half = slots_a.shape[0]
    spread_rows(-jnp.concatenate([square_rows(slots_a), square_rows(slots_b)], axis=0), wide_g)
    fill_scores(near, slots_a, score, 0)
    fill_scores(near, slots_b, score, half)
    row_pass(score, wide_g, peak, total, 0)
    to_places(row_result(peak, total), placed, range(LOT_SHARE // 2))
    placed[LOT_SHARE:, :] = lot_rows[...]


def far_score_kernel(slots_a, slots_b, wide_g, placed_before, *refs):
    parts, (score, far, out, placed, peak, total) = refs[: LOT_SHARE // 2], refs[LOT_SHARE // 2 :]
    gather_rows(parts, far)
    half = slots_a.shape[0]
    fill_scores(far, slots_a, score, 0)
    fill_scores(far, slots_b, score, half)
    row_pass(score, wide_g, peak, total, 0)
    placed[...] = placed_before[...]
    to_places(row_result(peak, total), placed, range(LOT_SHARE // 2, LOT_SHARE))
    send_to_lots(placed[...], out)


def row_of_each(gathered, shares, row):
    stride = gathered.shape[0] // shares
    return [gathered[n * stride + row : n * stride + row + 1, :] for n in range(shares)]


def log_sum_of(parts, shares, blocks):
    stride = parts.shape[0] // shares
    return joined([parts[n * stride : n * stride + blocks, :] for n in range(shares)])


def lot_update(parts, first, blocks):
    logs = jnp.concatenate(row_of_each(first, LOT_SHARE, blocks), axis=0)
    squares = jnp.concatenate(row_of_each(first, LOT_SHARE, blocks + 1), axis=0)
    pot = logs + squares - log_sum_of(parts, LOT_SHARE, blocks)
    return pot - squares


def own_core_first(rows):
    half = rows.shape[0] // 2
    low, high = rows[:half, :], rows[half:, :]
    ahead = lax.axis_index("core") == 0
    return jnp.concatenate([jnp.where(ahead, low, high), jnp.where(ahead, high, low)], axis=0)


def slot_update(parts, first, blocks):
    logs = own_core_first(jnp.concatenate(row_of_each(first, SLOT_SHARE, blocks), axis=0))
    return logs - log_sum_of(parts, SLOT_SHARE, blocks)


def column_kernel(score_n, score_f, parts, first, slot_rows, out, wide_f, placed, sums):
    placed[...] = lot_update(parts, first, LOT_SHARE)
    me = place_in_lots()
    for b, step in enumerate(STEPS):
        row = placed[pl.ds(me ^ step, 1), :]
        wide_f[b * LANES : (b + 1) * LANES, :] = jnp.broadcast_to(row, (LANES, LANES)).T
    column_pass([score_n, score_f], wide_f, sums)
    half = sums.shape[0] // 2
    mine, other = sums[:half, :], sums[half:, :]
    ahead = lax.axis_index("core") == 0
    extra = [slot_rows[...]] if out.shape[0] // SLOT_SHARE > sums.shape[0] else []
    same = jnp.concatenate([mine, other, *extra], axis=0)
    turned = jnp.concatenate([other, mine, *extra], axis=0)
    rows = same.shape[0]
    for n in range(SLOT_SHARE):
        low = n < SLOT_SHARE // 2
        out[n * rows : (n + 1) * rows, :] = jnp.where(ahead, same if low else turned, turned if low else same)


def row_kernel(score_n, score_f, parts, first, out, wide_g, placed, peak, total):
    spread_rows(slot_update(parts, first, score_n.shape[1] // LANES), wide_g)
    row_pass(score_n, wide_g, peak, total, 0)
    row_pass(score_f, wide_g, peak, total, score_n.shape[0])
    to_places(row_result(peak, total), placed, range(LOT_SHARE))
    send_to_lots(placed[...], out)


def final_kernel(score_n, score_f, parts, first, wide_f, near, far, slots_a, slots_b, out, wide_g, *work):
    tiles = score_n.shape[1] // LANES
    spread_rows(slot_update(parts, first, tiles), wide_g)
    half, below, rows_of = slots_a.shape[0], score_n.shape[0], work[0].shape[0]
    plans, row_sums = work[: len(work) // 2], work[len(work) // 2 :]
    me = place_in_lots()

    def fill_plan(c):
        score, base = (score_n, 0) if c * rows_of < below else (score_f, below)
        for start in range(0, rows_of, 16):
            at = c * rows_of + start
            shift = wide_f[at : at + 16, :]
            wholes = []
            for t in range(tiles):
                cols = slice(t * LANES, (t + 1) * LANES)
                both = jnp.concatenate([wide_g[t * 8 : (t + 1) * 8, :]] * 2, axis=0)
                term = jnp.exp2(score[at - base : at - base + 16, cols] + (shift + both))
                plans[c][start : start + 16, cols] = term.astype(jnp.bfloat16)
                wholes.append(term)
            whole = jnp.sum(in_pairs(jnp.add, wholes), axis=1, keepdims=True)
            row_sums[c][start : start + 16, :] = jnp.broadcast_to(whole, (16, LANES))

    def finish(c):
        lots, base = (near, 0) if c * rows_of < below else (far, below)
        at = c * rows_of
        step_cols = 256
        for start in range(0, lots.shape[1], step_cols):
            cols = slice(start, start + step_cols)
            moved = jnp.dot(plans[c][:, :half], slots_a[:, cols], preferred_element_type=jnp.float32)
            moved = moved + jnp.dot(plans[c][:, half:], slots_b[:, cols], preferred_element_type=jnp.float32)
            sums = jnp.concatenate([row_sums[c][...]] * (step_cols // LANES), axis=1)
            grad = sums * lots[at - base : at - base + rows_of, cols].astype(jnp.float32) - moved
            for n in range(rows_of // LANES):
                to = pl.ds(pl.multiple_of((me ^ STEPS[at // LANES + n]) * LANES, LANES), LANES)
                out[to, cols] = grad[n * LANES : (n + 1) * LANES, :].astype(out.dtype)

    fill_plan(0)
    for c in range(len(plans)):
        if c + 1 < len(plans):
            fill_plan(c + 1)
        finish(c)


def call(kernel, outs, scratch, cost, *args, grant=12):
    near = pl.BlockSpec(memory_space=pltpu.VMEM)
    return pl.pallas_call(
        kernel,
        out_shape=outs,
        in_specs=[near] * len(args),
        out_specs=[near] * len(outs),
        scratch_shapes=[pltpu.VMEM(*item) for item in scratch],
        compiler_params=pltpu.CompilerParams(vmem_limit_bytes=grant * 2**20),
        cost_estimate=pl.CostEstimate(flops=cost, bytes_accessed=0, transcendentals=cost // 1024),
    )(*args)


def exchange(values, members):
    return lax.all_to_all(values, ALL, 0, 0, tiled=True, axis_index_groups=members)


def to_place(values, d):
    return lax.ppermute(values, ALL, [(group[i], group[i ^ d]) for group in LOT_GROUPS for i in range(LOT_SHARE)])


def local(lot_features, slot_features, lot_mass, slot_mass):
    own_rows, width = lot_features.shape
    lot_mass = lot_mass.reshape(-1, LANES)
    slot_mass = slot_mass.reshape(-1, LANES)

    slots_a = exchange(jnp.tile(slot_features, (SLOT_SHARE // 2, 1)), CORE_SLOT_GROUPS)
    near = [lot_features] + [to_place(lot_features, d) for d in range(2, LOT_SHARE, 2)]
    far = [to_place(part, 1) for part in near]
    n, m = LOT_SHARE * own_rows, SLOT_SHARE * own_rows
    slot_blocks = m // LANES
    f32 = jnp.float32

    def shape(*dims, dtype=f32):
        return jax.ShapeDtypeStruct(dims, dtype)

    own_lots, lot_rows, slot_rows = call(
        own_kernel,
        [shape(own_rows, width, dtype=lot_features.dtype), shape(8, LANES), shape(8, LANES)],
        [],
        own_rows * width,
        lot_features, lot_mass, slot_mass,
    )
    slots_a, near[1], near[2], near[3], far[0], far[1], far[2], own_lots, lot_rows, slot_rows = lax.optimization_barrier(
        (slots_a, *near[1:], *far[:3], own_lots, lot_rows, slot_rows)
    )
    slots_b = lax.ppermute(slots_a, "core", [(0, 1), (1, 0)])

    wide_g, placed, wide_f, half_f = ((slot_blocks * 8, LANES), (LOT_SHARE, LANES), (n, LANES), (n // 2, LANES))
    work = n * m * 4

    half_lots = shape(n // 2, width, dtype=lot_features.dtype)
    score_n, near, g, placed_n = call(
        near_score_kernel,
        [shape(n // 2, m), half_lots, shape(*wide_g), shape(LOT_SHARE + 8, LANES)],
        [(half_f, f32), (half_f, f32)],
        work // 2,
        slots_a, slots_b, lot_rows, own_lots, *near[1:],
    )
    score_f, far, out = call(
        far_score_kernel,
        [shape(n // 2, m), half_lots, shape(LOT_SHARE * (LOT_SHARE + 8), LANES)],
        [((LOT_SHARE + 8, LANES), f32), (half_f, f32), (half_f, f32)],
        work // 2,
        slots_a, slots_b, g, placed_n, *far,
    )
    first_lot = lot_parts = exchange(out, LOT_GROUPS)
    first_slot = None
    for step in range(ITERS):
        extra = 8 if step == 0 else 0
        out, f = call(
            column_kernel,
            [shape(SLOT_SHARE * (slot_blocks + extra), LANES), shape(*wide_f)],
            [(placed, f32), ((slot_blocks, LANES), f32)],
            work,
            score_n, score_f, lot_parts, first_lot, slot_rows,
        )
        slot_parts = exchange(out, SLOT_GROUPS)
        if step == 0:
            first_slot = slot_parts
        if step < ITERS - 1:
            (out,) = call(
                row_kernel,
                [shape(LOT_SHARE * LOT_SHARE, LANES)],
                [(wide_g, f32), (placed, f32), (wide_f, f32), (wide_f, f32)],
                work,
                score_n, score_f, slot_parts, first_slot,
            )
            lot_parts = exchange(out, LOT_GROUPS)
    (partial,) = call(
        final_kernel,
        [shape(n, width, dtype=jnp.bfloat16)],
        [(wide_g, f32)] + [((n // CHUNKS, m), jnp.bfloat16)] * CHUNKS + [((n // CHUNKS, LANES), f32)] * CHUNKS,
        work,
        score_n, score_f, slot_parts, first_slot, f, near, far, slots_a, slots_b,
    )
    shares = exchange(partial, LOT_GROUPS).astype(f32)
    return jnp.sum(shares.reshape(LOT_SHARE, own_rows, width), axis=0)


def solution(mesh):
    fine = Mesh(mesh.devices.reshape(tuple(SIZES.values())), ALL)
    placed = (P(ALL, None), P(("x", "z", "y", "core"), None), P(("y", "core")), P(("x", "z")))
    return jax.shard_map(local, mesh=fine, in_specs=placed, out_specs=P(ALL, None), check_vma=False)
```

```python
import math

import jax
import jax.numpy as jnp
from jax import lax
from jax.experimental import pallas as pl
from jax.experimental.pallas import tpu as pltpu
from jax.sharding import Mesh, PartitionSpec as P

ITERS = 3
LOG2E = math.log2(math.e)
LANES = 128

SIZES = {"y": 4, "core": 2, "x": 4, "z": 4}
ALL = tuple(SIZES)
FULL, PAIRS, ACROSS, EACH = [(0, 1, 2, 3)], [(0, 1), (2, 3)], [(1, 2), (3, 0)], [(0,), (1,), (2,), (3,)]


def groups(ys, cores, xs, zs):
    return [
        [((y * 2 + core) * 4 + x) * 4 + z for core in cs for x in px for y in py for z in pz]
        for px in xs
        for py in ys
        for pz in zs
        for cs in cores
    ]


LOT_GROUPS = groups(EACH, [(0,), (1,)], FULL, PAIRS)
SLOT_GROUPS = groups(FULL, [(0, 1)], EACH, ACROSS)
CORE_SLOT_GROUPS = groups(FULL, [(0,), (1,)], EACH, ACROSS)
LOT_SHARE, SLOT_SHARE = 8, 16
CHUNKS = 2
ORDER = (1, 5, 3, 7, 4, 2, 6)


def place_in_lots():
    return lax.axis_index("x") * 2 + lax.axis_index("z") % 2


def lane_sum(values):
    total = values[:, :LANES]
    for start in range(LANES, values.shape[1], LANES):
        total = total + values[:, start : start + LANES]
    return jnp.sum(total.T, axis=0, keepdims=True)


def square_row(block):
    wide = block.astype(jnp.float32)
    return lane_sum(wide * wide) * (0.5 * LOG2E / math.sqrt(block.shape[1]))


def square_rows(features):
    return jnp.concatenate([square_row(features[start : start + LANES, :]) for start in range(0, features.shape[0], LANES)], axis=0)


def joined(parts):
    top = parts[0]
    for part in parts[1:]:
        top = jnp.maximum(top, part)
    total = jnp.exp2(parts[0] - top)
    for part in parts[1:]:
        total = total + jnp.exp2(part - top)
    return top + jnp.log(total) * LOG2E


def in_pairs(join, terms):
    while len(terms) > 1:
        terms = [join(*terms[i : i + 2]) if i + 1 < len(terms) else terms[i] for i in range(0, len(terms), 2)]
    return terms[0]


def peak_of(terms):
    return in_pairs(jnp.maximum, terms)


def fold(terms, top):
    return in_pairs(jnp.add, [jnp.exp2(term - top) for term in terms])


def onward(state, terms):
    top = peak_of(terms)
    if state is None:
        return top, fold(terms, top)
    top = jnp.maximum(top, state[0])
    return top, state[1] * jnp.exp2(state[0] - top) + fold(terms, top)


def row_pass(score, wide_g, peak, total, first):
    groups_of, tiles_of = 8, 8

    def step(i, carry):
        rows = [pl.multiple_of(i * 8 * groups_of + 8 * r, 8) for r in range(groups_of)]
        states = [None] * groups_of
        for start in range(0, score.shape[1] // LANES, tiles_of):
            gs = [wide_g[(start + k) * 8 : (start + k + 1) * 8, :] for k in range(tiles_of)]
            for r, row in enumerate(rows):
                terms = [score[pl.ds(row, 8), (start + k) * LANES : (start + k + 1) * LANES] + g for k, g in enumerate(gs)]
                states[r] = onward(states[r], terms)
        for row, (top, whole) in zip(rows, states, strict=True):
            peak[pl.ds(first + row, 8), :] = top
            total[pl.ds(first + row, 8), :] = whole
        return carry

    lax.fori_loop(0, score.shape[0] // (8 * groups_of), step, 0)


def row_result(peak, total):
    out = []
    for start in range(0, peak.shape[0], LANES):
        tops = peak[start : start + LANES, :].T
        sums = total[start : start + LANES, :].T
        top = jnp.max(tops, axis=0, keepdims=True)
        whole = jnp.sum(sums * jnp.exp2(tops - top), axis=0, keepdims=True)
        out.append(top + jnp.log(whole) * LOG2E)
    return jnp.concatenate(out, axis=0)


def column_pass(scores, wides, sums):
    rows, tiles_of = 64, 8
    below = scores[0].shape[0]

    def step(i, carry):
        cols = [pl.ds(pl.multiple_of((i * tiles_of + k) * LANES, LANES), LANES) for k in range(tiles_of)]
        states = [None] * tiles_of
        for start in range(0, below * len(scores), rows):
            score, wide_f, at = scores[start // below], wides[start // below], start % below
            fs = [wide_f[at + k : at + k + 8, :] for k in range(0, rows, 8)]
            for k, col in enumerate(cols):
                terms = [score[at + 8 * n : at + 8 * n + 8, col] + f for n, f in enumerate(fs)]
                states[k] = onward(states[k], terms)
        for k, (top, whole) in enumerate(states):
            high = jnp.max(top, axis=0, keepdims=True)
            whole = jnp.sum(whole * jnp.exp2(top - high), axis=0, keepdims=True)
            sums[pl.ds(i * tiles_of + k, 1), :] = high + jnp.log(whole) * LOG2E
        return carry

    lax.fori_loop(0, sums.shape[0] // tiles_of, step, 0)


def spread_rows(values, wide):
    for t in range(values.shape[0]):
        wide[t * 8 : (t + 1) * 8, :] = jnp.broadcast_to(values[t : t + 1, :], (8, LANES))


def padded(rows):
    have = jnp.concatenate(rows, axis=0)
    return jnp.concatenate([have, jnp.zeros((8 - have.shape[0], LANES), jnp.float32)], axis=0)


def fill_scores(lots, slots, score, first):
    scale = LOG2E / math.sqrt(lots.shape[1])
    step = 256
    for start in range(0, slots.shape[0], step):
        inner = lax.dot_general(
            lots[...], slots[start : start + step, :], (((1,), (1,)), ((), ())), preferred_element_type=jnp.float32
        )
        score[:, first + start : first + start + step] = inner * scale


STEPS = (0, 2, 4, 6, 1, 3, 5, 7)


def to_places(rows, placed, blocks):
    me = place_in_lots()
    for n, b in enumerate(blocks):
        placed[pl.ds(me ^ STEPS[b], 1), :] = rows[n : n + 1, :]


def send_to_lots(values, out):
    rows = values.shape[0]
    for n in range(LOT_SHARE):
        out[n * rows : (n + 1) * rows, :] = values


def gather_rows(parts, lots):
    rows = parts[0].shape[0]
    for n, part in enumerate(parts):
        lots[n * rows : (n + 1) * rows, :] = part[...]


def own_kernel(lots, lot_mass, slot_mass, own_lots, lot_rows, near_logs):
    own_lots[...] = lots[...]
    masses = lot_mass[pl.ds(lax.axis_index("x") * SIZES["z"] + lax.axis_index("z"), 1), :]
    lot_rows[...] = padded([jnp.log(masses) * LOG2E, square_row(lots[...])])
    near_logs[...] = jnp.log(slot_mass[...]) * LOG2E


def all_slot_logs(near_logs, across_logs):
    core, place = lax.axis_index("core"), (lax.axis_index("z") + 1) % 2
    rows = []
    for at in (core, 1 - core):
        for y in range(SIZES["y"]):
            row = pl.ds(y * SIZES["core"] + at, 1)
            rows += [jnp.where(place == z, near_logs[row, :], across_logs[row, :]) for z in range(2)]
    return jnp.concatenate(rows, axis=0)


def near_score_kernel(slots_a, slots_b, lot_rows, *refs):
    parts, (score, near, wide_g, placed, peak, total) = refs[: LOT_SHARE // 2], refs[LOT_SHARE // 2 :]
    gather_rows(parts, near)
    half = slots_a.shape[0]
    spread_rows(-jnp.concatenate([square_rows(slots_a), square_rows(slots_b)], axis=0), wide_g)
    fill_scores(near, slots_a, score, 0)
    fill_scores(near, slots_b, score, half)
    row_pass(score, wide_g, peak, total, 0)
    to_places(row_result(peak, total), placed, range(LOT_SHARE // 2))
    placed[LOT_SHARE:, :] = lot_rows[...]


def far_score_kernel(slots_a, slots_b, near_logs, across_logs, wide_g, placed_before, *refs):
    parts, (score, far, slot_logs, out, placed, peak, total) = refs[: LOT_SHARE // 2], refs[LOT_SHARE // 2 :]
    gather_rows(parts, far)
    slot_logs[...] = all_slot_logs(near_logs, across_logs)
    half = slots_a.shape[0]
    fill_scores(far, slots_a, score, 0)
    fill_scores(far, slots_b, score, half)
    row_pass(score, wide_g, peak, total, 0)
    placed[...] = placed_before[...]
    to_places(row_result(peak, total), placed, range(LOT_SHARE // 2, LOT_SHARE))
    send_to_lots(placed[...], out)


def row_of_each(gathered, shares, row):
    stride = gathered.shape[0] // shares
    return [gathered[n * stride + row : n * stride + row + 1, :] for n in range(shares)]


def log_sum_of(parts, shares, blocks):
    stride = parts.shape[0] // shares
    return joined([parts[n * stride : n * stride + blocks, :] for n in range(shares)])


def lot_update(parts, first, blocks):
    logs = jnp.concatenate(row_of_each(first, LOT_SHARE, blocks), axis=0)
    squares = jnp.concatenate(row_of_each(first, LOT_SHARE, blocks + 1), axis=0)
    pot = logs + squares - log_sum_of(parts, LOT_SHARE, blocks)
    return pot - squares


def slot_update(parts, slot_logs):
    return slot_logs[...] - log_sum_of(parts, SLOT_SHARE, slot_logs.shape[0])


def column_kernel(score_n, score_f, parts, first, out, wide_n, wide_far, placed, sums):
    placed[...] = lot_update(parts, first, LOT_SHARE)
    me = place_in_lots()
    for b, step in enumerate(STEPS):
        row = placed[pl.ds(me ^ step, 1), :]
        wide, at = (wide_n, b) if b < LOT_SHARE // 2 else (wide_far, b - LOT_SHARE // 2)
        wide[at * LANES : (at + 1) * LANES, :] = jnp.broadcast_to(row, (LANES, LANES)).T
    column_pass([score_n, score_f], [wide_n, wide_far], sums)
    half = sums.shape[0] // 2
    mine, other = sums[:half, :], sums[half:, :]
    ahead = lax.axis_index("core") == 0
    same, turned = sums[...], jnp.concatenate([other, mine], axis=0)
    rows = same.shape[0]
    for n in range(SLOT_SHARE):
        low = n < SLOT_SHARE // 2
        out[n * rows : (n + 1) * rows, :] = jnp.where(ahead, same if low else turned, turned if low else same)


def row_kernel(score_n, score_f, parts, slot_logs, out, wide_g, placed, peak, total):
    spread_rows(slot_update(parts, slot_logs), wide_g)
    row_pass(score_n, wide_g, peak, total, 0)
    row_pass(score_f, wide_g, peak, total, score_n.shape[0])
    to_places(row_result(peak, total), placed, range(LOT_SHARE))
    send_to_lots(placed[...], out)


def final_kernel(score, parts, slot_logs, wide_f, lots, slots_a, slots_b, *refs):
    blocks = score.shape[0] // LANES
    outs, wide_g, work = refs[:blocks], refs[blocks], refs[blocks + 1 :]
    tiles = score.shape[1] // LANES
    spread_rows(slot_update(parts, slot_logs), wide_g)
    half, rows_of = slots_a.shape[0], work[0].shape[0]
    plans, row_sums = work[: len(work) // 2], work[len(work) // 2 :]

    def fill_plan(c):
        for start in range(0, rows_of, 16):
            rows = slice(c * rows_of + start, c * rows_of + start + 16)
            shift = wide_f[rows, :]
            wholes = []
            for t in range(tiles):
                cols = slice(t * LANES, (t + 1) * LANES)
                both = jnp.concatenate([wide_g[t * 8 : (t + 1) * 8, :]] * 2, axis=0)
                term = jnp.exp2(score[rows, cols] + (shift + both))
                plans[c][start : start + 16, cols] = term.astype(jnp.bfloat16)
                wholes.append(term)
            whole = jnp.sum(in_pairs(jnp.add, wholes), axis=1, keepdims=True)
            row_sums[c][start : start + 16, :] = jnp.broadcast_to(whole, (16, LANES))

    def finish(c):
        at = c * rows_of
        step_cols = 256
        for start in range(0, lots.shape[1], step_cols):
            cols = slice(start, start + step_cols)
            moved = jnp.dot(plans[c][:, :half], slots_a[:, cols], preferred_element_type=jnp.float32)
            moved = moved + jnp.dot(plans[c][:, half:], slots_b[:, cols], preferred_element_type=jnp.float32)
            sums = jnp.concatenate([row_sums[c][...]] * (step_cols // LANES), axis=1)
            grad = sums * lots[at : at + rows_of, cols].astype(jnp.float32) - moved
            for n in range(rows_of // LANES):
                out = outs[at // LANES + n]
                out[:, cols] = grad[n * LANES : (n + 1) * LANES, :].astype(out.dtype)

    fill_plan(0)
    for c in range(len(plans)):
        if c + 1 < len(plans):
            fill_plan(c + 1)
        finish(c)


def call(kernel, outs, scratch, cost, *args, grant=12):
    near = pl.BlockSpec(memory_space=pltpu.VMEM)
    return pl.pallas_call(
        kernel,
        out_shape=outs,
        in_specs=[near] * len(args),
        out_specs=[near] * len(outs),
        scratch_shapes=[pltpu.VMEM(*item) for item in scratch],
        compiler_params=pltpu.CompilerParams(vmem_limit_bytes=grant * 2**20),
        cost_estimate=pl.CostEstimate(flops=cost, bytes_accessed=0, transcendentals=cost // 1024),
    )(*args)


def exchange(values, members):
    return lax.all_to_all(values, ALL, 0, 0, tiled=True, axis_index_groups=members)


def to_place(values, d):
    return lax.ppermute(values, ALL, [(group[i], group[i ^ d]) for group in LOT_GROUPS for i in range(LOT_SHARE)])


def local(lot_features, slot_features, lot_mass, slot_mass):
    own_rows, width = lot_features.shape
    lot_mass = lot_mass.reshape(-1, LANES)
    slot_mass = slot_mass.reshape(-1, LANES)

    slots_a = exchange(jnp.tile(slot_features, (SLOT_SHARE // 2, 1)), CORE_SLOT_GROUPS)
    near = [lot_features] + [to_place(lot_features, d) for d in range(2, LOT_SHARE, 2)]
    far = [to_place(part, 1) for part in near]
    n, m = LOT_SHARE * own_rows, SLOT_SHARE * own_rows
    slot_blocks = m // LANES
    f32 = jnp.float32

    def shape(*dims, dtype=f32):
        return jax.ShapeDtypeStruct(dims, dtype)

    own_lots, lot_rows, near_logs = call(
        own_kernel,
        [shape(own_rows, width, dtype=lot_features.dtype), shape(8, LANES), shape(slot_blocks // 2, LANES)],
        [],
        own_rows * width,
        lot_features, lot_mass, slot_mass,
    )
    slots_a, near[1], near[2], near[3], far[0], far[1], far[2], own_lots, lot_rows, near_logs = lax.optimization_barrier(
        (slots_a, *near[1:], *far[:3], own_lots, lot_rows, near_logs)
    )
    slots_b = lax.ppermute(slots_a, "core", [(0, 1), (1, 0)])
    across_logs = lax.ppermute(near_logs, "z", [(a, b) for pair in ACROSS for a, b in (pair, pair[::-1])])

    wide_g, placed, wide_f, half_f = ((slot_blocks * 8, LANES), (LOT_SHARE, LANES), (n, LANES), (n // 2, LANES))
    work = n * m * 4

    half_lots = shape(n // 2, width, dtype=lot_features.dtype)
    score_n, near, g, placed_n = call(
        near_score_kernel,
        [shape(n // 2, m), half_lots, shape(*wide_g), shape(LOT_SHARE + 8, LANES)],
        [(half_f, f32), (half_f, f32)],
        work // 2,
        slots_a, slots_b, lot_rows, own_lots, *near[1:],
    )
    score_f, far, slot_logs, out = call(
        far_score_kernel,
        [shape(n // 2, m), half_lots, shape(slot_blocks, LANES), shape(LOT_SHARE * (LOT_SHARE + 8), LANES)],
        [((LOT_SHARE + 8, LANES), f32), (half_f, f32), (half_f, f32)],
        work // 2,
        slots_a, slots_b, near_logs, across_logs, g, placed_n, *far,
    )
    first_lot = lot_parts = exchange(out, LOT_GROUPS)
    for step in range(ITERS):
        last = step == ITERS - 1
        halves = [half_f, half_f]
        out, *f_halves = call(
            column_kernel,
            [shape(SLOT_SHARE * slot_blocks, LANES)] + [shape(*dims) for dims in halves if last],
            [(dims, f32) for dims in halves if not last] + [(placed, f32), ((slot_blocks, LANES), f32)],
            work,
            score_n, score_f, lot_parts, first_lot,
        )
        slot_parts = exchange(out, SLOT_GROUPS)
        if not last:
            (out,) = call(
                row_kernel,
                [shape(LOT_SHARE * LOT_SHARE, LANES)],
                [(wide_g, f32), (placed, f32), (wide_f, f32), (wide_f, f32)],
                work,
                score_n, score_f, slot_parts, slot_logs,
            )
            lot_parts = exchange(out, LOT_GROUPS)
    parts = {}
    for score, lots, at in ((score_f, far, LOT_SHARE // 2), (score_n, near, 0)):
        steps = STEPS[at : at + LOT_SHARE // 2]
        outs = call(
            final_kernel,
            [shape(own_rows, width, dtype=jnp.bfloat16 if d else f32) for d in steps],
            [(wide_g, f32)] + [((n // 2 // CHUNKS, m), jnp.bfloat16)] * CHUNKS + [((n // 2 // CHUNKS, LANES), f32)] * CHUNKS,
            work // 2,
            score, slot_parts, slot_logs, f_halves[at // (LOT_SHARE // 2)], lots, slots_a, slots_b,
        )
        parts.update(zip(steps, outs, strict=True))
    arrived = [to_place(parts[d], d) for d in ORDER]
    return parts[0] + sum(part.astype(f32) for part in arrived)


def solution(mesh):
    fine = Mesh(mesh.devices.reshape(tuple(SIZES.values())), ALL)
    placed = (P(ALL, None), P(("x", "z", "y", "core"), None), P(("y", "core")), P(("x", "z")))
    return jax.shard_map(local, mesh=fine, in_specs=placed, out_specs=P(ALL, None), check_vma=False)
```

```python
import math

import jax
import jax.numpy as jnp
from jax import lax
from jax.experimental import pallas as pl
from jax.experimental.pallas import tpu as pltpu
from jax.sharding import Mesh, PartitionSpec as P

ITERS = 3
LOG2E = math.log2(math.e)
LANES = 128

SIZES = {"y": 4, "core": 2, "x": 4, "z": 4}
ALL = tuple(SIZES)
FULL, PAIRS, ACROSS, EACH = [(0, 1, 2, 3)], [(0, 1), (2, 3)], [(1, 2), (3, 0)], [(0,), (1,), (2,), (3,)]


def groups(ys, cores, xs, zs):
    return [
        [((y * 2 + core) * 4 + x) * 4 + z for core in cs for x in px for y in py for z in pz]
        for px in xs
        for py in ys
        for pz in zs
        for cs in cores
    ]


LOT_GROUPS = groups(EACH, [(0,), (1,)], FULL, PAIRS)
SLOT_GROUPS = groups(FULL, [(0, 1)], EACH, ACROSS)
CORE_SLOT_GROUPS = groups(FULL, [(0,), (1,)], EACH, ACROSS)
LOT_SHARE, SLOT_SHARE = 8, 16
CHUNKS = 2
ORDER = (1, 5, 3, 7, 4, 2, 6)


def place_in_lots():
    return lax.axis_index("x") * 2 + lax.axis_index("z") % 2


def lane_sum(values):
    total = values[:, :LANES]
    for start in range(LANES, values.shape[1], LANES):
        total = total + values[:, start : start + LANES]
    return jnp.sum(total.T, axis=0, keepdims=True)


def square_row(block):
    wide = block.astype(jnp.float32)
    return lane_sum(wide * wide) * (0.5 * LOG2E / math.sqrt(block.shape[1]))


def square_rows(features):
    return jnp.concatenate([square_row(features[start : start + LANES, :]) for start in range(0, features.shape[0], LANES)], axis=0)


def joined(parts):
    top = parts[0]
    for part in parts[1:]:
        top = jnp.maximum(top, part)
    total = jnp.exp2(parts[0] - top)
    for part in parts[1:]:
        total = total + jnp.exp2(part - top)
    return top + jnp.log(total) * LOG2E


def in_pairs(join, terms):
    while len(terms) > 1:
        terms = [join(*terms[i : i + 2]) if i + 1 < len(terms) else terms[i] for i in range(0, len(terms), 2)]
    return terms[0]


def peak_of(terms):
    return in_pairs(jnp.maximum, terms)


def fold(terms, top):
    return in_pairs(jnp.add, [jnp.exp2(term - top) for term in terms])


def onward(state, terms):
    top = peak_of(terms)
    if state is None:
        return top, fold(terms, top)
    top = jnp.maximum(top, state[0])
    return top, state[1] * jnp.exp2(state[0] - top) + fold(terms, top)


def row_pass(score, wide_g, peak, total, first):
    groups_of, tiles_of = 8, 8

    def step(i, carry):
        rows = [pl.multiple_of(i * 8 * groups_of + 8 * r, 8) for r in range(groups_of)]
        states = [None] * groups_of
        for start in range(0, score.shape[1] // LANES, tiles_of):
            gs = [wide_g[(start + k) * 8 : (start + k + 1) * 8, :] for k in range(tiles_of)]
            for r, row in enumerate(rows):
                terms = [score[pl.ds(row, 8), (start + k) * LANES : (start + k + 1) * LANES] + g for k, g in enumerate(gs)]
                states[r] = onward(states[r], terms)
        for row, (top, whole) in zip(rows, states, strict=True):
            peak[pl.ds(first + row, 8), :] = top
            total[pl.ds(first + row, 8), :] = whole
        return carry

    lax.fori_loop(0, score.shape[0] // (8 * groups_of), step, 0, unroll=4)


def row_result(peak, total):
    out = []
    for start in range(0, peak.shape[0], LANES):
        tops = peak[start : start + LANES, :].T
        sums = total[start : start + LANES, :].T
        top = jnp.max(tops, axis=0, keepdims=True)
        whole = jnp.sum(sums * jnp.exp2(tops - top), axis=0, keepdims=True)
        out.append(top + jnp.log(whole) * LOG2E)
    return jnp.concatenate(out, axis=0)


def column_pass(scores, wides, sums):
    rows, tiles_of = 64, 8
    below = scores[0].shape[0]

    def step(i, carry):
        cols = [pl.ds(pl.multiple_of((i * tiles_of + k) * LANES, LANES), LANES) for k in range(tiles_of)]
        states = [None] * tiles_of
        for start in range(0, below * len(scores), rows):
            score, wide_f, at = scores[start // below], wides[start // below], start % below
            fs = [wide_f[at + k : at + k + 8, :] for k in range(0, rows, 8)]
            for k, col in enumerate(cols):
                terms = [score[at + 8 * n : at + 8 * n + 8, col] + f for n, f in enumerate(fs)]
                states[k] = onward(states[k], terms)
        for k, (top, whole) in enumerate(states):
            high = jnp.max(top, axis=0, keepdims=True)
            whole = jnp.sum(whole * jnp.exp2(top - high), axis=0, keepdims=True)
            sums[pl.ds(i * tiles_of + k, 1), :] = high + jnp.log(whole) * LOG2E
        return carry

    lax.fori_loop(0, sums.shape[0] // tiles_of, step, 0, unroll=2)


def spread_rows(values, wide):
    for t in range(values.shape[0]):
        wide[t * 8 : (t + 1) * 8, :] = jnp.broadcast_to(values[t : t + 1, :], (8, LANES))


def padded(rows):
    have = jnp.concatenate(rows, axis=0)
    return jnp.concatenate([have, jnp.zeros((8 - have.shape[0], LANES), jnp.float32)], axis=0)


def fill_scores(lots, slots, score, first):
    scale = LOG2E / math.sqrt(lots.shape[1])
    step = 256
    for start in range(0, slots.shape[0], step):
        inner = lax.dot_general(
            lots[...], slots[start : start + step, :], (((1,), (1,)), ((), ())), preferred_element_type=jnp.float32
        )
        score[:, first + start : first + start + step] = inner * scale


STEPS = (0, 2, 4, 6, 1, 3, 5, 7)


def to_places(rows, placed, blocks):
    me = place_in_lots()
    for n, b in enumerate(blocks):
        placed[pl.ds(me ^ STEPS[b], 1), :] = rows[n : n + 1, :]


def send_to_lots(values, out):
    rows = values.shape[0]
    for n in range(LOT_SHARE):
        out[n * rows : (n + 1) * rows, :] = values


def gather_rows(parts, lots):
    rows = parts[0].shape[0]
    for n, part in enumerate(parts):
        lots[n * rows : (n + 1) * rows, :] = part[...]


def own_kernel(lots, lot_mass, slot_mass, own_lots, lot_rows, near_logs):
    own_lots[...] = lots[...]
    masses = lot_mass[pl.ds(lax.axis_index("x") * SIZES["z"] + lax.axis_index("z"), 1), :]
    lot_rows[...] = padded([jnp.log(masses) * LOG2E, square_row(lots[...])])
    near_logs[...] = jnp.log(slot_mass[...]) * LOG2E


def all_slot_logs(near_logs, across_logs):
    core, place = lax.axis_index("core"), (lax.axis_index("z") + 1) % 2
    rows = []
    for at in (core, 1 - core):
        for y in range(SIZES["y"]):
            row = pl.ds(y * SIZES["core"] + at, 1)
            rows += [jnp.where(place == z, near_logs[row, :], across_logs[row, :]) for z in range(2)]
    return jnp.concatenate(rows, axis=0)


def near_score_kernel(slots_a, slots_b, lot_rows, *refs):
    parts, (score, near, wide_g, placed, peak, total) = refs[: LOT_SHARE // 2], refs[LOT_SHARE // 2 :]
    gather_rows(parts, near)
    half = slots_a.shape[0]
    spread_rows(-jnp.concatenate([square_rows(slots_a), square_rows(slots_b)], axis=0), wide_g)
    fill_scores(near, slots_a, score, 0)
    fill_scores(near, slots_b, score, half)
    row_pass(score, wide_g, peak, total, 0)
    to_places(row_result(peak, total), placed, range(LOT_SHARE // 2))
    placed[LOT_SHARE:, :] = lot_rows[...]


def far_score_kernel(slots_a, slots_b, near_logs, across_logs, wide_g, placed_before, *refs):
    parts, (score, far, slot_logs, out, placed, peak, total) = refs[: LOT_SHARE // 2], refs[LOT_SHARE // 2 :]
    gather_rows(parts, far)
    slot_logs[...] = all_slot_logs(near_logs, across_logs)
    half = slots_a.shape[0]
    fill_scores(far, slots_a, score, 0)
    fill_scores(far, slots_b, score, half)
    row_pass(score, wide_g, peak, total, 0)
    placed[...] = placed_before[...]
    to_places(row_result(peak, total), placed, range(LOT_SHARE // 2, LOT_SHARE))
    send_to_lots(placed[...], out)


def row_of_each(gathered, shares, row):
    stride = gathered.shape[0] // shares
    return [gathered[n * stride + row : n * stride + row + 1, :] for n in range(shares)]


def log_sum_of(parts, shares, blocks):
    stride = parts.shape[0] // shares
    return joined([parts[n * stride : n * stride + blocks, :] for n in range(shares)])


def lot_update(parts, first, blocks):
    logs = jnp.concatenate(row_of_each(first, LOT_SHARE, blocks), axis=0)
    squares = jnp.concatenate(row_of_each(first, LOT_SHARE, blocks + 1), axis=0)
    pot = logs + squares - log_sum_of(parts, LOT_SHARE, blocks)
    return pot - squares


def slot_update(parts, slot_logs):
    return slot_logs[...] - log_sum_of(parts, SLOT_SHARE, slot_logs.shape[0])


def column_kernel(score_n, score_f, parts, first, out, wide_n, wide_far, placed, sums):
    placed[...] = lot_update(parts, first, LOT_SHARE)
    me = place_in_lots()
    for b, step in enumerate(STEPS):
        row = placed[pl.ds(me ^ step, 1), :]
        wide, at = (wide_n, b) if b < LOT_SHARE // 2 else (wide_far, b - LOT_SHARE // 2)
        wide[at * LANES : (at + 1) * LANES, :] = jnp.broadcast_to(row, (LANES, LANES)).T
    column_pass([score_n, score_f], [wide_n, wide_far], sums)
    half = sums.shape[0] // 2
    mine, other = sums[:half, :], sums[half:, :]
    ahead = lax.axis_index("core") == 0
    same, turned = sums[...], jnp.concatenate([other, mine], axis=0)
    rows = same.shape[0]
    for n in range(SLOT_SHARE):
        low = n < SLOT_SHARE // 2
        out[n * rows : (n + 1) * rows, :] = jnp.where(ahead, same if low else turned, turned if low else same)


def row_kernel(score_n, score_f, parts, slot_logs, out, wide_g, placed, peak, total):
    spread_rows(slot_update(parts, slot_logs), wide_g)
    row_pass(score_n, wide_g, peak, total, 0)
    row_pass(score_f, wide_g, peak, total, score_n.shape[0])
    to_places(row_result(peak, total), placed, range(LOT_SHARE))
    send_to_lots(placed[...], out)


def final_kernel(score, parts, slot_logs, wide_f, lots, slots_a, slots_b, *refs):
    blocks = score.shape[0] // LANES
    outs, wide_g, work = refs[:blocks], refs[blocks], refs[blocks + 1 :]
    tiles = score.shape[1] // LANES
    spread_rows(slot_update(parts, slot_logs), wide_g)
    half, rows_of = slots_a.shape[0], work[0].shape[0]
    plans, row_sums = work[: len(work) // 2], work[len(work) // 2 :]

    def fill_plan(c):
        for start in range(0, rows_of, 16):
            rows = slice(c * rows_of + start, c * rows_of + start + 16)
            shift = wide_f[rows, :]
            wholes = []
            for t in range(tiles):
                cols = slice(t * LANES, (t + 1) * LANES)
                both = jnp.concatenate([wide_g[t * 8 : (t + 1) * 8, :]] * 2, axis=0)
                term = jnp.exp2(score[rows, cols] + (shift + both))
                plans[c][start : start + 16, cols] = term.astype(jnp.bfloat16)
                wholes.append(term)
            whole = jnp.sum(in_pairs(jnp.add, wholes), axis=1, keepdims=True)
            row_sums[c][start : start + 16, :] = jnp.broadcast_to(whole, (16, LANES))

    def finish(c):
        at = c * rows_of
        step_cols = 256
        for start in range(0, lots.shape[1], step_cols):
            cols = slice(start, start + step_cols)
            moved = jnp.dot(plans[c][:, :half], slots_a[:, cols], preferred_element_type=jnp.float32)
            moved = moved + jnp.dot(plans[c][:, half:], slots_b[:, cols], preferred_element_type=jnp.float32)
            sums = jnp.concatenate([row_sums[c][...]] * (step_cols // LANES), axis=1)
            grad = sums * lots[at : at + rows_of, cols].astype(jnp.float32) - moved
            for n in range(rows_of // LANES):
                out = outs[at // LANES + n]
                out[:, cols] = grad[n * LANES : (n + 1) * LANES, :].astype(out.dtype)

    fill_plan(0)
    for c in range(len(plans)):
        if c + 1 < len(plans):
            fill_plan(c + 1)
        finish(c)


def call(kernel, outs, scratch, cost, *args, grant=12):
    near = pl.BlockSpec(memory_space=pltpu.VMEM)
    return pl.pallas_call(
        kernel,
        out_shape=outs,
        in_specs=[near] * len(args),
        out_specs=[near] * len(outs),
        scratch_shapes=[pltpu.VMEM(*item) for item in scratch],
        compiler_params=pltpu.CompilerParams(vmem_limit_bytes=grant * 2**20),
        cost_estimate=pl.CostEstimate(flops=cost, bytes_accessed=0, transcendentals=cost // 1024),
    )(*args)


def exchange(values, members):
    return lax.all_to_all(values, ALL, 0, 0, tiled=True, axis_index_groups=members)


def to_place(values, d):
    return lax.ppermute(values, ALL, [(group[i], group[i ^ d]) for group in LOT_GROUPS for i in range(LOT_SHARE)])


def local(lot_features, slot_features, lot_mass, slot_mass):
    own_rows, width = lot_features.shape
    lot_mass = lot_mass.reshape(-1, LANES)
    slot_mass = slot_mass.reshape(-1, LANES)

    slots_a = exchange(jnp.tile(slot_features, (SLOT_SHARE // 2, 1)), CORE_SLOT_GROUPS)
    near = [lot_features] + [to_place(lot_features, d) for d in range(2, LOT_SHARE, 2)]
    far = [to_place(part, 1) for part in near]
    n, m = LOT_SHARE * own_rows, SLOT_SHARE * own_rows
    slot_blocks = m // LANES
    f32 = jnp.float32

    def shape(*dims, dtype=f32):
        return jax.ShapeDtypeStruct(dims, dtype)

    own_lots, lot_rows, near_logs = call(
        own_kernel,
        [shape(own_rows, width, dtype=lot_features.dtype), shape(8, LANES), shape(slot_blocks // 2, LANES)],
        [],
        own_rows * width,
        lot_features, lot_mass, slot_mass,
    )
    slots_a, near[1], near[2], near[3], far[0], far[1], far[2], own_lots, lot_rows, near_logs = lax.optimization_barrier(
        (slots_a, *near[1:], *far[:3], own_lots, lot_rows, near_logs)
    )
    slots_b = lax.ppermute(slots_a, "core", [(0, 1), (1, 0)])
    across_logs = lax.ppermute(near_logs, "z", [(a, b) for pair in ACROSS for a, b in (pair, pair[::-1])])

    wide_g, placed, wide_f, half_f = ((slot_blocks * 8, LANES), (LOT_SHARE, LANES), (n, LANES), (n // 2, LANES))
    work = n * m * 4

    half_lots = shape(n // 2, width, dtype=lot_features.dtype)
    score_n, near, g, placed_n = call(
        near_score_kernel,
        [shape(n // 2, m), half_lots, shape(*wide_g), shape(LOT_SHARE + 8, LANES)],
        [(half_f, f32), (half_f, f32)],
        work // 2,
        slots_a, slots_b, lot_rows, own_lots, *near[1:],
    )
    score_f, far, slot_logs, out = call(
        far_score_kernel,
        [shape(n // 2, m), half_lots, shape(slot_blocks, LANES), shape(LOT_SHARE * (LOT_SHARE + 8), LANES)],
        [((LOT_SHARE + 8, LANES), f32), (half_f, f32), (half_f, f32)],
        work // 2,
        slots_a, slots_b, near_logs, across_logs, g, placed_n, *far,
    )
    first_lot = lot_parts = exchange(out, LOT_GROUPS)
    for step in range(ITERS):
        last = step == ITERS - 1
        halves = [half_f, half_f]
        out, *f_halves = call(
            column_kernel,
            [shape(SLOT_SHARE * slot_blocks, LANES)] + [shape(*dims) for dims in halves if last],
            [(dims, f32) for dims in halves if not last] + [(placed, f32), ((slot_blocks, LANES), f32)],
            work,
            score_n, score_f, lot_parts, first_lot,
        )
        slot_parts = exchange(out, SLOT_GROUPS)
        if not last:
            (out,) = call(
                row_kernel,
                [shape(LOT_SHARE * LOT_SHARE, LANES)],
                [(wide_g, f32), (placed, f32), (wide_f, f32), (wide_f, f32)],
                work,
                score_n, score_f, slot_parts, slot_logs,
            )
            lot_parts = exchange(out, LOT_GROUPS)
    parts = {}
    for score, lots, at in ((score_f, far, LOT_SHARE // 2), (score_n, near, 0)):
        steps = STEPS[at : at + LOT_SHARE // 2]
        outs = call(
            final_kernel,
            [shape(own_rows, width, dtype=jnp.bfloat16 if d else f32) for d in steps],
            [(wide_g, f32)] + [((n // 2 // CHUNKS, m), jnp.bfloat16)] * CHUNKS + [((n // 2 // CHUNKS, LANES), f32)] * CHUNKS,
            work // 2,
            score, slot_parts, slot_logs, f_halves[at // (LOT_SHARE // 2)], lots, slots_a, slots_b,
        )
        parts.update(zip(steps, outs, strict=True))
    arrived = [to_place(parts[d], d) for d in ORDER]
    return parts[0] + sum(part.astype(f32) for part in arrived)


def solution(mesh):
    fine = Mesh(mesh.devices.reshape(tuple(SIZES.values())), ALL)
    placed = (P(ALL, None), P(("x", "z", "y", "core"), None), P(("y", "core")), P(("x", "z")))
    return jax.shard_map(local, mesh=fine, in_specs=placed, out_specs=P(ALL, None), check_vma=False)
```

```python
import math

import jax
import jax.numpy as jnp
from jax import lax
from jax.experimental import pallas as pl
from jax.experimental.pallas import tpu as pltpu
from jax.sharding import Mesh, PartitionSpec as P

ITERS = 3
LOG2E = math.log2(math.e)
LANES = 128

SIZES = {"y": 4, "core": 2, "x": 4, "z": 4}
ALL = tuple(SIZES)
FULL, PAIRS, ACROSS, EACH = [(0, 1, 2, 3)], [(0, 1), (2, 3)], [(1, 2), (3, 0)], [(0,), (1,), (2,), (3,)]


def groups(ys, cores, xs, zs):
    return [
        [((y * 2 + core) * 4 + x) * 4 + z for core in cs for x in px for y in py for z in pz]
        for px in xs
        for py in ys
        for pz in zs
        for cs in cores
    ]


LOT_GROUPS = groups(EACH, [(0,), (1,)], FULL, PAIRS)
SLOT_GROUPS = groups(FULL, [(0, 1)], EACH, ACROSS)
CORE_SLOT_GROUPS = groups(FULL, [(0,), (1,)], EACH, ACROSS)
LOT_SHARE, SLOT_SHARE = 8, 16
CHUNKS = 2
ORDER = (1, 5, 3, 7, 4, 2, 6)


def place_in_lots():
    return lax.axis_index("x") * 2 + lax.axis_index("z") % 2


def lane_sum(values):
    total = values[:, :LANES]
    for start in range(LANES, values.shape[1], LANES):
        total = total + values[:, start : start + LANES]
    return jnp.sum(total.T, axis=0, keepdims=True)


def square_row(block):
    wide = block.astype(jnp.float32)
    return lane_sum(wide * wide) * (0.5 * LOG2E / math.sqrt(block.shape[1]))


def square_rows(features):
    return jnp.concatenate([square_row(features[start : start + LANES, :]) for start in range(0, features.shape[0], LANES)], axis=0)


def joined(parts):
    top = parts[0]
    for part in parts[1:]:
        top = jnp.maximum(top, part)
    total = jnp.exp2(parts[0] - top)
    for part in parts[1:]:
        total = total + jnp.exp2(part - top)
    return top + jnp.log(total) * LOG2E


def in_pairs(join, terms):
    while len(terms) > 1:
        terms = [join(*terms[i : i + 2]) if i + 1 < len(terms) else terms[i] for i in range(0, len(terms), 2)]
    return terms[0]


def peak_of(terms):
    return in_pairs(jnp.maximum, terms)


def fold(terms, top):
    return in_pairs(jnp.add, [jnp.exp2(term - top) for term in terms])


def onward(state, terms):
    top = peak_of(terms)
    if state is None:
        return top, fold(terms, top)
    top = jnp.maximum(top, state[0])
    return top, state[1] * jnp.exp2(state[0] - top) + fold(terms, top)


def row_pass(score, wide_g, peak, total, first):
    groups_of, tiles_of = 8, 8

    def step(i, carry):
        rows = [pl.multiple_of(i * 8 * groups_of + 8 * r, 8) for r in range(groups_of)]
        states = [None] * groups_of
        for start in range(0, score.shape[1] // LANES, tiles_of):
            gs = [wide_g[(start + k) * 8 : (start + k + 1) * 8, :] for k in range(tiles_of)]
            for r, row in enumerate(rows):
                terms = [score[pl.ds(row, 8), (start + k) * LANES : (start + k + 1) * LANES] + g for k, g in enumerate(gs)]
                states[r] = onward(states[r], terms)
        for row, (top, whole) in zip(rows, states, strict=True):
            peak[pl.ds(first + row, 8), :] = top
            total[pl.ds(first + row, 8), :] = whole
        return carry

    lax.fori_loop(0, score.shape[0] // (8 * groups_of), step, 0, unroll=4)


def row_result(peak, total):
    out = []
    for start in range(0, peak.shape[0], LANES):
        tops = peak[start : start + LANES, :].T
        sums = total[start : start + LANES, :].T
        top = jnp.max(tops, axis=0, keepdims=True)
        whole = jnp.sum(sums * jnp.exp2(tops - top), axis=0, keepdims=True)
        out.append(top + jnp.log(whole) * LOG2E)
    return jnp.concatenate(out, axis=0)


def column_pass(scores, wides, sums):
    rows, tiles_of = 64, 8
    below = scores[0].shape[0]

    def step(i, carry):
        cols = [pl.ds(pl.multiple_of((i * tiles_of + k) * LANES, LANES), LANES) for k in range(tiles_of)]
        states = [None] * tiles_of
        for start in range(0, below * len(scores), rows):
            score, wide_f, at = scores[start // below], wides[start // below], start % below
            fs = [wide_f[at + k : at + k + 8, :] for k in range(0, rows, 8)]
            for k, col in enumerate(cols):
                terms = [score[at + 8 * n : at + 8 * n + 8, col] + f for n, f in enumerate(fs)]
                states[k] = onward(states[k], terms)
        for k, (top, whole) in enumerate(states):
            high = jnp.max(top, axis=0, keepdims=True)
            whole = jnp.sum(whole * jnp.exp2(top - high), axis=0, keepdims=True)
            sums[pl.ds(i * tiles_of + k, 1), :] = high + jnp.log(whole) * LOG2E
        return carry

    lax.fori_loop(0, sums.shape[0] // tiles_of, step, 0, unroll=2)


def spread_rows(values, wide):
    for t in range(values.shape[0]):
        wide[t * 8 : (t + 1) * 8, :] = jnp.broadcast_to(values[t : t + 1, :], (8, LANES))


def padded(rows):
    have = jnp.concatenate(rows, axis=0)
    return jnp.concatenate([have, jnp.zeros((8 - have.shape[0], LANES), jnp.float32)], axis=0)


def fill_scores(lots, slots, score, first):
    scale = LOG2E / math.sqrt(lots.shape[1])
    step = 256
    for start in range(0, slots.shape[0], step):
        inner = lax.dot_general(
            lots[...], slots[start : start + step, :], (((1,), (1,)), ((), ())), preferred_element_type=jnp.float32
        )
        score[:, first + start : first + start + step] = inner * scale


STEPS = (0, 2, 4, 6, 1, 3, 5, 7)


def to_places(rows, placed, blocks):
    me = place_in_lots()
    for n, b in enumerate(blocks):
        placed[pl.ds(me ^ STEPS[b], 1), :] = rows[n : n + 1, :]


def send_to_lots(values, out):
    rows = values.shape[0]
    for n in range(LOT_SHARE):
        out[n * rows : (n + 1) * rows, :] = values


def gather_rows(parts, lots):
    rows = parts[0].shape[0]
    for n, part in enumerate(parts):
        lots[n * rows : (n + 1) * rows, :] = part[...]


def own_kernel(lots, lot_mass, slot_mass, own_lots, lot_rows, near_logs):
    own_lots[...] = lots[...]
    masses = lot_mass[pl.ds(lax.axis_index("x") * SIZES["z"] + lax.axis_index("z"), 1), :]
    lot_rows[...] = padded([jnp.log(masses) * LOG2E, square_row(lots[...])])
    near_logs[...] = jnp.log(slot_mass[...]) * LOG2E


def all_slot_logs(near_logs, across_logs):
    core, place = lax.axis_index("core"), (lax.axis_index("z") + 1) % 2
    rows = []
    for at in (core, 1 - core):
        for y in range(SIZES["y"]):
            row = pl.ds(y * SIZES["core"] + at, 1)
            rows += [jnp.where(place == z, near_logs[row, :], across_logs[row, :]) for z in range(2)]
    return jnp.concatenate(rows, axis=0)


def near_score_kernel(slots_a, slots_b, lot_rows, *refs):
    parts, (score, near, wide_g, placed, peak, total) = refs[: LOT_SHARE // 2], refs[LOT_SHARE // 2 :]
    gather_rows(parts, near)
    half = slots_a.shape[0]
    spread_rows(-jnp.concatenate([square_rows(slots_a), square_rows(slots_b)], axis=0), wide_g)
    fill_scores(near, slots_a, score, 0)
    fill_scores(near, slots_b, score, half)
    row_pass(score, wide_g, peak, total, 0)
    to_places(row_result(peak, total), placed, range(LOT_SHARE // 2))
    placed[LOT_SHARE:, :] = lot_rows[...]


def far_score_kernel(slots_a, slots_b, near_logs, across_logs, wide_g, placed_before, *refs):
    parts, (score, far, slot_logs, out, placed, peak, total) = refs[: LOT_SHARE // 2], refs[LOT_SHARE // 2 :]
    gather_rows(parts, far)
    slot_logs[...] = all_slot_logs(near_logs, across_logs)
    half = slots_a.shape[0]
    fill_scores(far, slots_a, score, 0)
    fill_scores(far, slots_b, score, half)
    row_pass(score, wide_g, peak, total, 0)
    placed[...] = placed_before[...]
    to_places(row_result(peak, total), placed, range(LOT_SHARE // 2, LOT_SHARE))
    send_to_lots(placed[...], out)


def row_of_each(gathered, shares, row):
    stride = gathered.shape[0] // shares
    return [gathered[n * stride + row : n * stride + row + 1, :] for n in range(shares)]


def log_sum_of(parts, shares, blocks):
    stride = parts.shape[0] // shares
    return joined([parts[n * stride : n * stride + blocks, :] for n in range(shares)])


def lot_update(parts, first, blocks):
    logs = jnp.concatenate(row_of_each(first, LOT_SHARE, blocks), axis=0)
    squares = jnp.concatenate(row_of_each(first, LOT_SHARE, blocks + 1), axis=0)
    pot = logs + squares - log_sum_of(parts, LOT_SHARE, blocks)
    return pot - squares


def slot_update(parts, slot_logs):
    return slot_logs[...] - log_sum_of(parts, SLOT_SHARE, slot_logs.shape[0])


def column_kernel(score_n, score_f, parts, first, out, wide_n, wide_far, placed, sums):
    placed[...] = lot_update(parts, first, LOT_SHARE)
    me = place_in_lots()
    for b, step in enumerate(STEPS):
        row = placed[pl.ds(me ^ step, 1), :]
        wide, at = (wide_n, b) if b < LOT_SHARE // 2 else (wide_far, b - LOT_SHARE // 2)
        wide[at * LANES : (at + 1) * LANES, :] = jnp.broadcast_to(row, (LANES, LANES)).T
    column_pass([score_n, score_f], [wide_n, wide_far], sums)
    half = sums.shape[0] // 2
    mine, other = sums[:half, :], sums[half:, :]
    ahead = lax.axis_index("core") == 0
    same, turned = sums[...], jnp.concatenate([other, mine], axis=0)
    rows = same.shape[0]
    for n in range(SLOT_SHARE):
        low = n < SLOT_SHARE // 2
        out[n * rows : (n + 1) * rows, :] = jnp.where(ahead, same if low else turned, turned if low else same)


def row_kernel(score_n, score_f, parts, slot_logs, out, wide_g, placed, peak, total):
    spread_rows(slot_update(parts, slot_logs), wide_g)
    row_pass(score_n, wide_g, peak, total, 0)
    row_pass(score_f, wide_g, peak, total, score_n.shape[0])
    to_places(row_result(peak, total), placed, range(LOT_SHARE))
    send_to_lots(placed[...], out)


def final_kernel(score, parts, slot_logs, wide_f, lots, slots_a, slots_b, *refs):
    blocks = score.shape[0] // LANES
    outs, wide_g, work = refs[:blocks], refs[blocks], refs[blocks + 1 :]
    tiles = score.shape[1] // LANES
    spread_rows(slot_update(parts, slot_logs), wide_g)
    half, rows_of = slots_a.shape[0], work[0].shape[0]
    plans, row_sums = work[: len(work) // 2], work[len(work) // 2 :]

    def fill_plan(c):
        for start in range(0, rows_of, 16):
            rows = slice(c * rows_of + start, c * rows_of + start + 16)
            shift = wide_f[rows, :]
            wholes = []
            for t in range(tiles):
                cols = slice(t * LANES, (t + 1) * LANES)
                both = jnp.concatenate([wide_g[t * 8 : (t + 1) * 8, :]] * 2, axis=0)
                term = jnp.exp2(score[rows, cols] + (shift + both))
                plans[c][start : start + 16, cols] = term.astype(jnp.bfloat16)
                wholes.append(term)
            whole = jnp.sum(in_pairs(jnp.add, wholes), axis=1, keepdims=True)
            row_sums[c][start : start + 16, :] = jnp.broadcast_to(whole, (16, LANES))

    def finish(c):
        at = c * rows_of
        step_cols = 256
        for start in range(0, lots.shape[1], step_cols):
            cols = slice(start, start + step_cols)
            moved = jnp.dot(plans[c][:, :half], slots_a[:, cols], preferred_element_type=jnp.float32)
            moved = moved + jnp.dot(plans[c][:, half:], slots_b[:, cols], preferred_element_type=jnp.float32)
            sums = jnp.concatenate([row_sums[c][...]] * (step_cols // LANES), axis=1)
            grad = sums * lots[at : at + rows_of, cols].astype(jnp.float32) - moved
            for n in range(rows_of // LANES):
                out = outs[at // LANES + n]
                out[:, cols] = grad[n * LANES : (n + 1) * LANES, :].astype(out.dtype)

    fill_plan(0)
    for c in range(len(plans)):
        if c + 1 < len(plans):
            fill_plan(c + 1)
        finish(c)


def call(kernel, outs, scratch, cost, *args, grant=12):
    near = pl.BlockSpec(memory_space=pltpu.VMEM)
    return pl.pallas_call(
        kernel,
        out_shape=outs,
        in_specs=[near] * len(args),
        out_specs=[near] * len(outs),
        scratch_shapes=[pltpu.VMEM(*item) for item in scratch],
        compiler_params=pltpu.CompilerParams(vmem_limit_bytes=grant * 2**20),
        cost_estimate=pl.CostEstimate(flops=cost, bytes_accessed=0, transcendentals=cost // 1024),
    )(*args)


def exchange(values, members):
    return lax.all_to_all(values, ALL, 0, 0, tiled=True, axis_index_groups=members)


def to_place(values, d):
    return lax.ppermute(values, ALL, [(group[i], group[i ^ d]) for group in LOT_GROUPS for i in range(LOT_SHARE)])


def local(lot_features, slot_features, lot_mass, slot_mass):
    own_rows, width = lot_features.shape
    lot_mass = lot_mass.reshape(-1, LANES)
    slot_mass = slot_mass.reshape(-1, LANES)

    slots_a = exchange(jnp.tile(slot_features, (SLOT_SHARE // 2, 1)), CORE_SLOT_GROUPS)
    near = [lot_features] + [to_place(lot_features, d) for d in range(2, LOT_SHARE, 2)]
    far = [to_place(part, 1) for part in near]
    n, m = LOT_SHARE * own_rows, SLOT_SHARE * own_rows
    slot_blocks = m // LANES
    f32 = jnp.float32

    def shape(*dims, dtype=f32):
        return jax.ShapeDtypeStruct(dims, dtype)

    own_lots, lot_rows, near_logs = call(
        own_kernel,
        [shape(own_rows, width, dtype=lot_features.dtype), shape(8, LANES), shape(slot_blocks // 2, LANES)],
        [],
        own_rows * width,
        lot_features, lot_mass, slot_mass,
    )
    slots_a, near[1], near[2], near[3], far[0], far[1], far[2], own_lots, lot_rows, near_logs = lax.optimization_barrier(
        (slots_a, *near[1:], *far[:3], own_lots, lot_rows, near_logs)
    )
    slots_b = lax.ppermute(slots_a, "core", [(0, 1), (1, 0)])
    across_logs = lax.ppermute(near_logs, "z", [(a, b) for pair in ACROSS for a, b in (pair, pair[::-1])])

    wide_g, placed, wide_f, half_f = ((slot_blocks * 8, LANES), (LOT_SHARE, LANES), (n, LANES), (n // 2, LANES))
    work = n * m * 4

    half_lots = shape(n // 2, width, dtype=lot_features.dtype)
    score_n, near, g, placed_n = call(
        near_score_kernel,
        [shape(n // 2, m), half_lots, shape(*wide_g), shape(LOT_SHARE + 8, LANES)],
        [(half_f, f32), (half_f, f32)],
        work // 2,
        slots_a, slots_b, lot_rows, own_lots, *near[1:],
    )
    score_f, far, slot_logs, out = call(
        far_score_kernel,
        [shape(n // 2, m), half_lots, shape(slot_blocks, LANES), shape(LOT_SHARE * (LOT_SHARE + 8), LANES)],
        [((LOT_SHARE + 8, LANES), f32), (half_f, f32), (half_f, f32)],
        work // 2,
        slots_a, slots_b, near_logs, across_logs, g, placed_n, *far,
    )
    first_lot = lot_parts = exchange(out, LOT_GROUPS)
    for step in range(ITERS):
        last = step == ITERS - 1
        halves = [half_f, half_f]
        out, *f_halves = call(
            column_kernel,
            [shape(SLOT_SHARE * slot_blocks, LANES)] + [shape(*dims) for dims in halves if last],
            [(dims, f32) for dims in halves if not last] + [(placed, f32), ((slot_blocks, LANES), f32)],
            work,
            score_n, score_f, lot_parts, first_lot,
        )
        slot_parts = exchange(out, SLOT_GROUPS)
        if not last:
            (out,) = call(
                row_kernel,
                [shape(LOT_SHARE * LOT_SHARE, LANES)],
                [(wide_g, f32), (placed, f32), (wide_f, f32), (wide_f, f32)],
                work,
                score_n, score_f, slot_parts, slot_logs,
            )
            lot_parts = exchange(out, LOT_GROUPS)
    parts = {}
    for score, lots, at in ((score_f, far, LOT_SHARE // 2), (score_n, near, 0)):
        steps = STEPS[at : at + LOT_SHARE // 2]
        outs = call(
            final_kernel,
            [shape(own_rows, width, dtype=jnp.bfloat16 if d else f32) for d in steps],
            [(wide_g, f32)] + [((n // 2 // CHUNKS, m), jnp.bfloat16)] * CHUNKS + [((n // 2 // CHUNKS, LANES), f32)] * CHUNKS,
            work // 2,
            score, slot_parts, slot_logs, f_halves[at // (LOT_SHARE // 2)], lots, slots_a, slots_b,
        )
        parts.update(zip(steps, outs, strict=True))
    arrived = [to_place(parts[d], d) for d in ORDER]
    early = lax.optimization_barrier(parts[0] + sum(part.astype(f32) for part in arrived[:4]))
    return early + sum(part.astype(f32) for part in arrived[4:])


def solution(mesh):
    fine = Mesh(mesh.devices.reshape(tuple(SIZES.values())), ALL)
    placed = (P(ALL, None), P(("x", "z", "y", "core"), None), P(("y", "core")), P(("x", "z")))
    return jax.shard_map(local, mesh=fine, in_specs=placed, out_specs=P(ALL, None), check_vma=False)
```
